512 devices in a mesh: seq: 128 (over x, z, core), ctx: 4 (over y).
Axes of the slice: x: 4, y: 4, z: 16, core: 2. Of those that a mesh axis runs over, the one named last changes fastest.
Arguments:
- hidden_rows: bfloat16 [128, 256, 8192], P('seq', 'ctx'), may hold values from -6 to 6
- chosen_query_rows: bfloat16 [128, 256, 8192], P('seq', 'ctx'), may hold values from -160 to 160
- key_rows: bfloat16 [128, 256, 1024], P('seq', 'ctx'), may hold values from -7 to 7
- chosen_value_rows: bfloat16 [128, 256, 1024], P('seq', 'ctx'), may hold values from -6 to 6
- output_gradient: bfloat16 [128, 256, 8192], P('seq', 'ctx'), may hold values from -6 to 6
- positions: int32 [128, 256], P('seq', 'ctx'), may hold values from 0 to 2048, as said below
- counts: int32 [128, 4], P('seq', 'ctx'), may hold values from 16 to 64, as said below
- router: float32 [8192], replicated, may hold values from -0.0625 to 0.0625
Outputs:
- query_gradient: bfloat16 [128, 256, 8192], P('seq', 'ctx')
- key_gradient: bfloat16 [128, 256, 1024], P('seq', 'ctx')
- value_gradient: bfloat16 [128, 256, 1024], P('seq', 'ctx')
- router_grad: float32 [8192], replicated
The draws below stay inside these ranges and needn't reach their ends.
Inputs may be any that keep to these rules, and one draw needn't show every extreme that they name: `counts`: some device holds 64 live rows in every draw. On device j of ctx, slots 0 to counts - 1 hold distinct increasing positions from j * 512 to (j + 1) * 512 - 1; the other slots hold 2048.
All inputs are finite; a program needn't handle non-finite values.
Results may differ from the reference program's by a relative error of at most 0.024.
Values may be sent and summed in bfloat16 or wider, within the bound.
No kernel may reach another device: no remote copies, remote signals or barrier semaphores. Data moves between devices by JAX's collectives and lax.ppermute only.
A program may use at most 64 MiB of HBM per device.

```python
import math
import jax
import jax.numpy as jnp
from jax import lax

D = 8192
QUERY_HEADS = 64
KEY_VALUE_HEADS = 8
HEAD_SIZE = 128
ROW_SLOTS = 64
TOK_DEV = 512
SEQ_LEN = 2048
N_SEQ = 128
N_CTX = 4


def shared_keys(key):
    return jnp.clip(jax.random.normal(key, (N_SEQ, N_CTX * ROW_SLOTS, KEY_VALUE_HEADS * HEAD_SIZE), jnp.float32), -6.0, 6.0)


def chosen_counts(key):
    inner = jax.random.fold_in(key, 7)
    start_offset = jax.random.randint(inner, (N_SEQ * N_CTX,), ROW_SLOTS // 4, ROW_SLOTS + 1)
    spot = jax.random.randint(jax.random.fold_in(key, 8), (), 0, N_SEQ * N_CTX)
    start_offset = jnp.where(jnp.arange(N_SEQ * N_CTX) == spot, ROW_SLOTS, start_offset)
    return start_offset.reshape(N_SEQ, N_CTX).astype(jnp.int32)


def draw_key_rows(key, part):
    start_offset = shared_keys(key)
    return start_offset.astype(jnp.bfloat16)


def draw_chosen_query_rows(key, part):
    key = jax.random.fold_in(key, 5)
    return jnp.clip(jax.random.normal(key, (N_SEQ, N_CTX * ROW_SLOTS, QUERY_HEADS * HEAD_SIZE), jnp.float32), -6.0, 6.0).astype(jnp.bfloat16)


def draw_counts(key, part):
    shared = chosen_counts(key)
    return shared


def pick_offsets(subkey):
    return jax.random.permutation(subkey, TOK_DEV)[:ROW_SLOTS]


def draw_positions(key, part):
    shared = chosen_counts(key)
    key = jax.random.fold_in(key, 13)
    subkeys = jax.random.split(key, N_SEQ * N_CTX)
    offsets = jax.vmap(pick_offsets)(subkeys)
    flat_counts = shared.reshape(-1)
    live = jnp.arange(ROW_SLOTS)[None, :] < flat_counts[:, None]
    ordered = jnp.sort(jnp.where(live, offsets, TOK_DEV), axis=1)
    starts = (jnp.arange(N_SEQ * N_CTX) % N_CTX * TOK_DEV)[:, None]
    placed = jnp.where(live, ordered + starts, SEQ_LEN)
    return placed.reshape(N_SEQ, N_CTX * ROW_SLOTS).astype(jnp.int32)


def block_levels(own_key, dims, pieces, least, top_value):
    gain = 1.0
    for dim, blocks in pieces:
        draws = jax.random.uniform(jax.random.fold_in(jax.random.fold_in(own_key, 6), dim), (blocks,), jnp.float32, least / len(pieces), top_value / len(pieces))
        gain = gain * jnp.repeat(jnp.exp(draws), dims[dim] // blocks).reshape((-1,) + (1,) * (len(dims) - 1 - dim))
    return gain


def gaussian(rng, dims, scale, most, shards=(), kind=jnp.bfloat16):
    values = jax.random.normal(rng, dims, jnp.float32) * scale
    if len(shards) > 0:
        values = block_levels(rng, dims, shards, -0.22, 0.18) * values
    return jnp.clip(values, min=-most, max=most).astype(kind)


def setup_inputs(seed: int = 0) -> dict:
    seeds = jax.random.split(jax.random.key(seed), 9)
    hidden_rows = gaussian(seeds[0], (N_SEQ, N_CTX * ROW_SLOTS, D), 1.0, 6.0, ((0, 128), (1, 4)))
    chosen_query_rows = draw_chosen_query_rows(jax.random.fold_in(seeds[8], 71), 0)
    key_rows = draw_key_rows(jax.random.fold_in(seeds[8], 71), 0)
    chosen_value_rows = gaussian(seeds[3], (N_SEQ, N_CTX * ROW_SLOTS, KEY_VALUE_HEADS * HEAD_SIZE), 1.0, 6.0, ((0, 128), (1, 4)))
    output_gradient = gaussian(seeds[4], (N_SEQ, N_CTX * ROW_SLOTS, QUERY_HEADS * HEAD_SIZE), 1.0, 6.0, ((0, 128), (1, 4)))
    positions = draw_positions(jax.random.fold_in(seeds[8], 71), 0)
    counts = draw_counts(jax.random.fold_in(seeds[8], 71), 0)
    router = gaussian(seeds[7], (D,), D ** -0.5, 0.0625, (), jnp.float32)
    return dict(hidden_rows=hidden_rows, chosen_query_rows=chosen_query_rows, key_rows=key_rows, chosen_value_rows=chosen_value_rows, output_gradient=output_gradient, positions=positions, counts=counts, router=router)


def reference(hidden_rows, chosen_query_rows, key_rows, chosen_value_rows, output_gradient, positions, counts, router):
    scale = 1.0 / math.sqrt(HEAD_SIZE)
    query_group_width = QUERY_HEADS // KEY_VALUE_HEADS
    single_float = jnp.float32

    def one_sequence(items):
        hidden, query_matrix, sequence_keys, sequence_values, sequence_gradients, places, chosen = items
        grand_total = query_matrix.shape[0]
        slot = jnp.arange(grand_total) % ROW_SLOTS
        shard = jnp.arange(grand_total) // ROW_SLOTS
        valid = (slot < chosen[shard]).astype(single_float)
        hidden_f = hidden.astype(single_float)
        logits = jnp.dot(hidden_f, router, precision=lax.Precision.HIGHEST)
        sigma = jax.nn.sigmoid(logits)
        gate = sigma * valid
        query_head_rows = query_matrix.reshape(grand_total, KEY_VALUE_HEADS, query_group_width, HEAD_SIZE).astype(single_float)
        key_head_rows = sequence_keys.reshape(grand_total, KEY_VALUE_HEADS, HEAD_SIZE).astype(single_float)
        value_head_rows = sequence_values.reshape(grand_total, KEY_VALUE_HEADS, HEAD_SIZE).astype(single_float)
        scores = jnp.einsum('qhgd,khd->hgqk', query_head_rows, key_head_rows) * scale
        allowed = places[None, :] <= places[:, None]
        scores = jnp.where(allowed, scores, -1e+30)
        row_max = lax.optimization_barrier(jnp.max(scores, axis=-1))
        weights = jnp.exp(scores - row_max[..., None])
        row_sum = lax.optimization_barrier(jnp.sum(weights, axis=-1))
        probs = (weights / row_sum[..., None]).astype(jnp.bfloat16).astype(single_float)
        attended = jnp.einsum('hgqk,khd->qhgd', probs, value_head_rows)
        gradient_list = sequence_gradients.reshape(grand_total, KEY_VALUE_HEADS, query_group_width, HEAD_SIZE).astype(single_float)
        grad_attended = (gate[:, None, None, None] * gradient_list).astype(jnp.bfloat16).astype(single_float)
        logit_grad = lax.optimization_barrier(jnp.sum(gradient_list * attended, axis=(1, 2, 3))) * sigma * (1.0 - sigma) * valid
        router_factor = jnp.dot(logit_grad, hidden_f, precision=lax.Precision.HIGHEST)
        value_gradient = jnp.einsum('hgqk,qhgd->khd', probs, grad_attended)
        grad_probs = jnp.einsum('qhgd,khd->hgqk', grad_attended, value_head_rows)
        row_dot = jnp.transpose(lax.optimization_barrier(jnp.sum(grad_attended * attended, axis=-1)), (1, 2, 0))
        grad_scores = (probs * (grad_probs - row_dot[..., None])).astype(jnp.bfloat16).astype(single_float)
        query_gradient = jnp.einsum('hgqk,khd->qhgd', grad_scores, key_head_rows) * scale
        key_gradient = jnp.einsum('hgqk,qhgd->khd', grad_scores, query_head_rows) * scale
        return (query_gradient.reshape(grand_total, QUERY_HEADS * HEAD_SIZE).astype(jnp.bfloat16), key_gradient.reshape(grand_total, KEY_VALUE_HEADS * HEAD_SIZE).astype(jnp.bfloat16), value_gradient.reshape(grand_total, KEY_VALUE_HEADS * HEAD_SIZE).astype(jnp.bfloat16), router_factor)
    query_gradient, key_gradient, value_gradient, terms = lax.map(one_sequence, (hidden_rows, chosen_query_rows, key_rows, chosen_value_rows, output_gradient, positions, counts))
    router_grad = lax.optimization_barrier(jnp.sum(terms, axis=0)) / math.sqrt(N_SEQ * N_CTX * ROW_SLOTS)
    return (query_gradient, key_gradient, value_gradient, router_grad)
```

```python
import functools
import math

import jax
import jax.numpy as jnp
from jax import lax
from jax.experimental import pallas as pl
from jax.experimental.pallas import tpu as pltpu
from jax.sharding import Mesh, PartitionSpec as P

QUERY_HEADS = 64
KEY_VALUE_HEADS = 8
HEAD_SIZE = 128
GROUP = QUERY_HEADS // KEY_VALUE_HEADS
KV_WIDTH = KEY_VALUE_HEADS * HEAD_SIZE
SCALE = 1.0 / math.sqrt(HEAD_SIZE)
LOG2_SCALE = SCALE * math.log2(math.e)
X, Z, CORES, Y = 4, 16, 2, 4
PLANE = X * CORES * Y
VMEM_LIMIT = 48 * 1024 * 1024
NT = (((1,), (1,)), ((), ()))
TN = (((0,), (0,)), ((), ()))
NN = (((1,), (0,)), ((), ()))


def dot(a, b, dims):
    return lax.dot_general(a, b, dims, preferred_element_type=jnp.float32)


def params():
    return pltpu.CompilerParams(vmem_limit_bytes=VMEM_LIMIT)


def column(row, rows):
    wide = jnp.broadcast_to(row, (rows, rows))
    diagonal = lax.broadcasted_iota(jnp.int32, (rows, rows), 0) == lax.broadcasted_iota(
        jnp.int32, (rows, rows), 1
    )
    return jnp.sum(jnp.where(diagonal, wide.astype(jnp.float32), 0.0), axis=1, keepdims=True)


def pack_kernel(key_ref, value_ref, place_ref, out_ref):
    rows = key_ref.shape[1]
    places = column(place_ref[...], rows)
    high = jnp.floor(places * (1.0 / 16.0))
    low = places - 16.0 * high
    lane = lax.broadcasted_iota(jnp.int32, (rows, 128), 1)
    coded = jnp.where(lane == 0, high, jnp.where(lane == 1, low, 0.0)).astype(jnp.bfloat16)
    for part in range(Y):
        out_ref[part, :, :KV_WIDTH] = key_ref[0]
        out_ref[part, :, KV_WIDTH : 2 * KV_WIDTH] = value_ref[0]
        out_ref[part, :, 2 * KV_WIDTH :] = coded


def gate_kernel(hidden_ref, router_ref, count_ref, gate_ref, slope_ref):
    rows, width = hidden_ref.shape[1:]
    step = 1024
    total = jnp.zeros((rows, 128), jnp.float32)
    for start in range(0, width, step):
        product = hidden_ref[0, :, start : start + step].astype(jnp.float32) * router_ref[
            :, start : start + step
        ]
        for piece in range(0, step, 128):
            total = total + product[:, piece : piece + 128]
    logits = jnp.sum(total, axis=1, keepdims=True)
    sigma = jax.nn.sigmoid(logits)
    slot = lax.broadcasted_iota(jnp.int32, (rows, 1), 0)
    valid = (slot < count_ref[0, 0]).astype(jnp.float32)
    gate_ref[...] = jnp.broadcast_to(sigma * valid, (rows, 128))
    slope_ref[...] = jnp.broadcast_to(sigma * (1.0 - sigma) * valid, (rows, 128))


def key_places(place_block):
    coded = place_block.reshape(-1, 128).astype(jnp.float32)
    return coded[:, 0:1] * 16.0 + coded[:, 1:2]


def stack_heads(block, first, rows):
    return jnp.concatenate(
        [block[:, (first + g) * HEAD_SIZE : (first + g + 1) * HEAD_SIZE] for g in range(GROUP)],
        axis=0,
    )


def weights_of(keys, queries, allowed):
    scores = jnp.where(allowed, dot(keys, queries, NT), -1e30)
    top = jnp.max(scores, axis=0, keepdims=True)
    weights = jnp.exp2((scores - top) * LOG2_SCALE)
    return weights, jnp.sum(weights, axis=0, keepdims=True)


def forward_kernel(
    heads, q_ref, grad_ref, k_ref, v_ref, kp_ref, qp_ref, slope_ref, hidden_ref, out_ref, acc_ref
):
    step = pl.program_id(0)
    rows = q_ref.shape[1]
    across = GROUP * rows

    @pl.when(step == 0)
    def _():
        acc_ref[...] = jnp.zeros_like(acc_ref)

    allowed = key_places(kp_ref[...]) <= qp_ref[...].astype(jnp.float32)
    for c in range(heads):
        queries = stack_heads(q_ref[0], c * GROUP, rows)
        grads = stack_heads(grad_ref[0], c * GROUP, rows)
        keys = k_ref[:, :, c * HEAD_SIZE : (c + 1) * HEAD_SIZE].reshape(-1, HEAD_SIZE)
        values = v_ref[:, :, c * HEAD_SIZE : (c + 1) * HEAD_SIZE].reshape(-1, HEAD_SIZE)
        weights, total = weights_of(keys, queries, allowed)
        along = dot(values, grads, NT)
        acc_ref[...] += jnp.sum(weights * along, axis=0, keepdims=True) / total

    @pl.when(step == pl.num_programs(0) - 1)
    def _():
        per_head = acc_ref[...]
        row_sum = per_head[:, :rows]
        for g in range(1, GROUP):
            row_sum = row_sum + per_head[:, g * rows : (g + 1) * rows]
        wide = jnp.broadcast_to(row_sum, (rows, rows))
        diagonal = lax.broadcasted_iota(jnp.int32, (rows, rows), 0) == lax.broadcasted_iota(
            jnp.int32, (rows, rows), 1
        )
        down = jnp.sum(jnp.where(diagonal, wide, 0.0), axis=1, keepdims=True)
        logit_grad = down * slope_ref[:, :1] * (1.0 / math.sqrt(X * Z * CORES * Y * rows))
        chunk = out_ref.shape[2]
        for part in range(PLANE):
            block = hidden_ref[0, :, part * chunk : (part + 1) * chunk].astype(jnp.float32)
            out_ref[part] = jnp.sum(block * logit_grad, axis=0, keepdims=True)


def backward_kernel(
    heads, q_ref, grad_ref, k_ref, v_ref, kp_ref, qp_ref, gate_ref, dq_ref, dk_ref, dv_ref
):
    rows = q_ref.shape[1]
    blocks = k_ref.shape[0]
    allowed = key_places(kp_ref[...]) <= qp_ref[...].astype(jnp.float32)
    gate = gate_ref[:, :1]
    for c in range(heads):
        queries = stack_heads(q_ref[0], c * GROUP, rows)
        grads = jnp.concatenate(
            [
                (
                    grad_ref[
                        0, :, (c * GROUP + g) * HEAD_SIZE : (c * GROUP + g + 1) * HEAD_SIZE
                    ].astype(jnp.float32)
                    * gate
                ).astype(jnp.bfloat16)
                for g in range(GROUP)
            ],
            axis=0,
        )
        own = slice(c * HEAD_SIZE, (c + 1) * HEAD_SIZE)
        keys = k_ref[:, :, own].reshape(-1, HEAD_SIZE)
        values = v_ref[:, :, own].reshape(-1, HEAD_SIZE)
        weights, total = weights_of(keys, queries, allowed)
        probs = (weights * (1.0 / total)).astype(jnp.bfloat16)
        probs32 = probs.astype(jnp.float32)
        grad_probs = dot(values, grads, NT)
        row_dot = jnp.sum(probs32 * grad_probs, axis=0, keepdims=True)
        grad_scores = (probs32 * (grad_probs - row_dot)).astype(jnp.bfloat16)
        dv = dot(probs, grads, NN)
        dk = dot(grad_scores, queries, NN) * SCALE
        dq = dot(grad_scores, keys, TN) * SCALE
        dv_ref[:, :, own] = dv.astype(jnp.bfloat16).reshape(blocks, rows, HEAD_SIZE)
        dk_ref[:, :, own] = dk.astype(jnp.bfloat16).reshape(blocks, rows, HEAD_SIZE)
        dq = dq.astype(jnp.bfloat16)
        for g in range(GROUP):
            left = (c * GROUP + g) * HEAD_SIZE
            dq_ref[0, :, left : left + HEAD_SIZE] = dq[g * rows : (g + 1) * rows]


def body(
    hidden_rows,
    chosen_query_rows,
    key_rows,
    chosen_value_rows,
    output_gradient,
    positions,
    counts,
    router,
):
    rows, width = chosen_query_rows.shape[1:]
    payload = pl.pallas_call(
        pack_kernel,
        out_shape=jax.ShapeDtypeStruct((Y, rows, 2 * KV_WIDTH + 128), jnp.bfloat16),
        compiler_params=params(),
        name="pack",
    )(key_rows, chosen_value_rows, positions)
    gathered = lax.all_to_all(payload, "ctx", 0, 0, tiled=True)

    gate, slope = pl.pallas_call(
        gate_kernel,
        out_shape=[jax.ShapeDtypeStruct((rows, 128), jnp.float32)] * 2,
        in_specs=[
            pl.BlockSpec(memory_space=pltpu.VMEM),
            pl.BlockSpec(memory_space=pltpu.VMEM),
            pl.BlockSpec(memory_space=pltpu.SMEM),
        ],
        compiler_params=params(),
        cost_estimate=pl.CostEstimate(
            flops=2 * rows * width, bytes_accessed=2 * rows * width, transcendentals=rows
        ),
        name="gate",
    )(hidden_rows, router.reshape(1, width), counts)

    query_places = jnp.tile(positions, (1, GROUP))
    heads = 2
    steps = KEY_VALUE_HEADS // heads
    span = heads * HEAD_SIZE
    wide_block = pl.BlockSpec((1, rows, heads * GROUP * HEAD_SIZE), lambda i: (0, 0, i))
    key_block = pl.BlockSpec((Y, rows, span), lambda i: (0, 0, i))
    value_block = pl.BlockSpec((Y, rows, span), lambda i: (0, 0, i + steps))
    place_block = pl.BlockSpec((Y, rows, 128), lambda i: (0, 0, 2 * KEY_VALUE_HEADS))

    def whole(*shape):
        return pl.BlockSpec(shape, lambda i: (0,) * len(shape))

    chunk = width // PLANE
    term = pl.pallas_call(
        functools.partial(forward_kernel, heads),
        grid=(steps,),
        out_shape=jax.ShapeDtypeStruct((PLANE, 1, chunk), jnp.float32),
        in_specs=[
            wide_block,
            wide_block,
            key_block,
            value_block,
            place_block,
            whole(1, GROUP * rows),
            whole(rows, 128),
            whole(1, rows, width),
        ],
        out_specs=whole(PLANE, 1, chunk),
        scratch_shapes=[pltpu.VMEM((1, GROUP * rows), jnp.float32)],
        compiler_params=params(),
        cost_estimate=pl.CostEstimate(
            flops=4 * rows * width * Y * rows,
            bytes_accessed=6 * rows * width,
            transcendentals=rows * QUERY_HEADS * Y * rows,
        ),
        name="forward",
    )(
        chosen_query_rows,
        output_gradient,
        gathered,
        gathered,
        gathered,
        query_places,
        slope,
        hidden_rows,
    )

    plane = ("x", "core", "ctx")
    shares = lax.all_to_all(term, plane, 0, 0, tiled=True)
    share = jnp.sum(shares, axis=0, keepdims=True)
    lines = lax.all_to_all(jnp.broadcast_to(share, (Z, 1, chunk)), "z", 0, 0, tiled=True)
    line = jnp.sum(lines, axis=0, keepdims=True)
    router_grad = lax.all_to_all(
        jnp.broadcast_to(line, (PLANE, 1, chunk)), plane, 0, 0, tiled=True
    ).reshape(width)

    part = pl.BlockSpec((Y, rows, span), lambda i: (0, 0, i))
    query_gradient, key_terms, value_terms = pl.pallas_call(
        functools.partial(backward_kernel, heads),
        grid=(steps,),
        out_shape=[
            jax.ShapeDtypeStruct((1, rows, width), jnp.bfloat16),
            jax.ShapeDtypeStruct((Y, rows, KV_WIDTH), jnp.bfloat16),
            jax.ShapeDtypeStruct((Y, rows, KV_WIDTH), jnp.bfloat16),
        ],
        in_specs=[
            wide_block,
            wide_block,
            key_block,
            value_block,
            place_block,
            whole(1, GROUP * rows),
            whole(rows, 128),
        ],
        out_specs=[wide_block, part, part],
        compiler_params=params(),
        cost_estimate=pl.CostEstimate(
            flops=10 * rows * width * Y * rows,
            bytes_accessed=6 * rows * width,
            transcendentals=rows * QUERY_HEADS * Y * rows,
        ),
        name="backward",
    )(
        chosen_query_rows,
        output_gradient,
        gathered,
        gathered,
        gathered,
        query_places,
        gate,
    )
    key_shares = lax.all_to_all(key_terms, "ctx", 0, 0, tiled=True)
    value_shares = lax.all_to_all(value_terms, "ctx", 0, 0, tiled=True)
    key_gradient = jnp.sum(key_shares.astype(jnp.float32), axis=0, keepdims=True)
    value_gradient = jnp.sum(value_shares.astype(jnp.float32), axis=0, keepdims=True)
    return (
        query_gradient,
        key_gradient.astype(jnp.bfloat16),
        value_gradient.astype(jnp.bfloat16),
        router_grad,
    )


def solution(mesh):
    fine = Mesh(mesh.devices.reshape(X, Z, CORES, Y), ("x", "z", "core", "ctx"))
    seq = ("x", "z", "core")
    rows3 = P(seq, "ctx", None)
    rows2 = P(seq, "ctx")
    return jax.shard_map(
        body,
        mesh=fine,
        in_specs=(rows3, rows3, rows3, rows3, rows3, rows2, rows2, P()),
        out_specs=(rows3, rows3, rows3, P()),
        check_vma=False,
    )
```

```python
import functools
import math

import jax
import jax.numpy as jnp
from jax import lax
from jax.experimental import pallas as pl
from jax.experimental.pallas import tpu as pltpu
from jax.sharding import Mesh, PartitionSpec as P

QUERY_HEADS = 64
KEY_VALUE_HEADS = 8
HEAD_SIZE = 128
GROUP = QUERY_HEADS // KEY_VALUE_HEADS
KV_WIDTH = KEY_VALUE_HEADS * HEAD_SIZE
SCALE = 1.0 / math.sqrt(HEAD_SIZE)
LOG2_SCALE = SCALE * math.log2(math.e)
X, Z, CORES, Y = 4, 16, 2, 4
PLANE = X * CORES * Y
VMEM_LIMIT = 48 * 1024 * 1024
FULL_VMEM = 60 * 1024 * 1024
FOLD_FLOPS = 1 << 35
HBM = pl.BlockSpec(memory_space=pltpu.HBM)
NT = (((1,), (1,)), ((), ()))
TN = (((0,), (0,)), ((), ()))
NN = (((1,), (0,)), ((), ()))


def dot(a, b, dims):
    return lax.dot_general(a, b, dims, preferred_element_type=jnp.float32)


def params(limit=VMEM_LIMIT):
    return pltpu.CompilerParams(vmem_limit_bytes=limit)


def column(row, rows):
    wide = jnp.broadcast_to(row, (rows, rows))
    diagonal = lax.broadcasted_iota(jnp.int32, (rows, rows), 0) == lax.broadcasted_iota(
        jnp.int32, (rows, rows), 1
    )
    return jnp.sum(jnp.where(diagonal, wide.astype(jnp.float32), 0.0), axis=1, keepdims=True)


def pack_kernel(key_ref, value_ref, place_ref, out_ref, row_ref, block_ref, in_sems, out_sems):
    rows = key_ref.shape[1]
    fetches = [
        pltpu.make_async_copy(place_ref, row_ref, in_sems.at[0]),
        pltpu.make_async_copy(key_ref.at[0], block_ref.at[:, :KV_WIDTH], in_sems.at[1]),
        pltpu.make_async_copy(
            value_ref.at[0], block_ref.at[:, KV_WIDTH : 2 * KV_WIDTH], in_sems.at[2]
        ),
    ]
    for fetch in fetches:
        fetch.start()
    fetches[0].wait()
    places = column(row_ref[...], rows)
    high = jnp.floor(places * (1.0 / 16.0))
    low = places - 16.0 * high
    lane = lax.broadcasted_iota(jnp.int32, (rows, 128), 1)
    coded = jnp.where(lane == 0, high, jnp.where(lane == 1, low, 0.0))
    block_ref[:, 2 * KV_WIDTH :] = coded.astype(jnp.bfloat16)
    fetches[1].wait()
    fetches[2].wait()
    copies = [
        pltpu.make_async_copy(block_ref, out_ref.at[part], out_sems.at[part]) for part in range(Y)
    ]
    for copy in copies:
        copy.start()
    for copy in copies:
        copy.wait()


def gate_kernel(hidden_ref, router_ref, count_ref, gate_ref, slope_ref):
    rows, width = hidden_ref.shape[1:]
    step = 1024
    total = jnp.zeros((rows, 128), jnp.float32)
    for start in range(0, width, step):
        product = hidden_ref[0, :, start : start + step].astype(jnp.float32) * router_ref[
            :, start : start + step
        ]
        for piece in range(0, step, 128):
            total = total + product[:, piece : piece + 128]
    logits = jnp.sum(total, axis=1, keepdims=True)
    sigma = jax.nn.sigmoid(logits)
    slot = lax.broadcasted_iota(jnp.int32, (rows, 1), 0)
    valid = (slot < count_ref[0, 0]).astype(jnp.float32)
    gate_ref[...] = jnp.broadcast_to(sigma * valid, (rows, 128))
    slope_ref[...] = jnp.broadcast_to(sigma * (1.0 - sigma) * valid, (rows, 128))


def key_places(place_block):
    coded = place_block.reshape(-1, 128).astype(jnp.float32)
    return coded[:, 0:1] * 16.0 + coded[:, 1:2]


def stack_heads(block, first, rows):
    return jnp.concatenate(
        [block[:, (first + g) * HEAD_SIZE : (first + g + 1) * HEAD_SIZE] for g in range(GROUP)],
        axis=0,
    )


def mask_bias(places, query_places):
    return jnp.where(places <= query_places.astype(jnp.float32), 0.0, -1e30)


def weights_of(keys, queries, bias):
    copies = GROUP * 64 // bias.shape[1]
    scores = dot(keys, queries, NT) + jnp.concatenate([bias] * copies, axis=1)
    top = jnp.max(scores, axis=0, keepdims=True)
    weights = jnp.exp2((scores - top) * LOG2_SCALE)
    return weights, jnp.sum(weights, axis=0, keepdims=True)


def forward_kernel(q_ref, grad_ref, pay_ref, qp_ref, out_ref):
    rows = q_ref.shape[1]
    bias = mask_bias(key_places(pay_ref[:, :, 2 * KV_WIDTH :]), qp_ref[:, : 2 * rows])
    acc = jnp.zeros((1, GROUP * rows), jnp.float32)
    for c in range(KEY_VALUE_HEADS):
        left = c * HEAD_SIZE
        queries = stack_heads(q_ref[0], c * GROUP, rows)
        grads = stack_heads(grad_ref[0], c * GROUP, rows)
        keys = pay_ref[:, :, left : left + HEAD_SIZE].reshape(-1, HEAD_SIZE)
        left = left + KV_WIDTH
        values = pay_ref[:, :, left : left + HEAD_SIZE].reshape(-1, HEAD_SIZE)
        weights, total = weights_of(keys, queries, bias)
        along = dot(values, grads, NT)
        acc = acc + jnp.sum(weights * along, axis=0, keepdims=True) / total
    row_sum = acc[:, :rows]
    for g in range(1, GROUP):
        row_sum = row_sum + acc[:, g * rows : (g + 1) * rows]
    wide = jnp.broadcast_to(row_sum, (rows, rows))
    diagonal = lax.broadcasted_iota(jnp.int32, (rows, rows), 0) == lax.broadcasted_iota(
        jnp.int32, (rows, rows), 1
    )
    down = jnp.sum(jnp.where(diagonal, wide, 0.0), axis=1, keepdims=True)
    out_ref[...] = jnp.broadcast_to(down, (rows, 128))


def router_kernel(along_ref, slope_ref, hidden_ref, out_ref):
    rows, chunk = hidden_ref.shape[1], out_ref.shape[2]
    logit_grad = along_ref[...] * slope_ref[...] * (1.0 / math.sqrt(X * Z * CORES * Y * rows))
    for part in range(PLANE):
        for lane in range(0, chunk, 128):
            left = part * chunk + lane
            block = hidden_ref[0, :, left : left + 128].astype(jnp.float32)
            out_ref[part, :, lane : lane + 128] = jnp.sum(
                block * logit_grad, axis=0, keepdims=True
            )


def backward_kernel(
    heads,
    q_ref,
    grad_ref,
    k_ref,
    v_ref,
    kp_ref,
    qp_ref,
    gate_ref,
    dq_ref,
    *term_refs,
):
    rows = q_ref.shape[1]
    me = lax.axis_index("ctx")
    owners = [lax.rem(me + Y - back, Y) for back in range(Y)]

    def blocks(ref, columns):
        return jnp.concatenate([ref[owner, :, columns] for owner in owners], axis=0)

    bias = mask_bias(key_places(blocks(kp_ref, slice(0, 128))), qp_ref[:, : 2 * rows])
    gate = gate_ref[:, :1]
    for c in range(heads):
        queries = stack_heads(q_ref[0], c * GROUP, rows)
        grads = jnp.concatenate(
            [
                (
                    grad_ref[
                        0, :, (c * GROUP + g) * HEAD_SIZE : (c * GROUP + g + 1) * HEAD_SIZE
                    ].astype(jnp.float32)
                    * gate
                ).astype(jnp.bfloat16)
                for g in range(GROUP)
            ],
            axis=0,
        )
        own = slice(c * HEAD_SIZE, (c + 1) * HEAD_SIZE)
        beside = slice((heads + c) * HEAD_SIZE, (heads + c + 1) * HEAD_SIZE)
        keys = blocks(k_ref, own)
        values = blocks(v_ref, own)
        weights, total = weights_of(keys, queries, bias)
        probs = (weights * (1.0 / total)).astype(jnp.bfloat16)
        probs32 = probs.astype(jnp.float32)
        grad_probs = dot(values, grads, NT)
        row_dot = jnp.sum(probs32 * grad_probs, axis=0, keepdims=True)
        grad_scores = (probs32 * (grad_probs - row_dot)).astype(jnp.bfloat16)
        dv = dot(probs, grads, NN).astype(jnp.bfloat16)
        dk = (dot(grad_scores, queries, NN) * SCALE).astype(jnp.bfloat16)
        dq = (dot(grad_scores, keys, TN) * SCALE).astype(jnp.bfloat16)
        for back, term_ref in enumerate(term_refs):
            term_ref[:, own] = dk[back * rows : (back + 1) * rows]
            term_ref[:, beside] = dv[back * rows : (back + 1) * rows]
        for g in range(GROUP):
            left = (c * GROUP + g) * HEAD_SIZE
            dq_ref[0, :, left : left + HEAD_SIZE] = dq[g * rows : (g + 1) * rows]


def combine_kernel(span, *refs):
    share_refs, (dk_ref, dv_ref) = refs[:-2], refs[-2:]
    total = share_refs[0][...].astype(jnp.float32)
    for share_ref in share_refs[1:]:
        total = total + share_ref[...].astype(jnp.float32)
    total = total.astype(jnp.bfloat16)
    for i in range(KV_WIDTH // span):
        own = slice(i * span, (i + 1) * span)
        dk_ref[0, :, own] = total[:, 2 * i * span : (2 * i + 1) * span]
        dv_ref[0, :, own] = total[:, (2 * i + 1) * span : (2 * i + 2) * span]


def fold_kernel(share_ref, out_ref):
    total = share_ref[0]
    for part in range(1, share_ref.shape[0]):
        total = total + share_ref[part]
    for part in range(out_ref.shape[0]):
        out_ref[part] = total


def fold(shares, parts, flops):
    return pl.pallas_call(
        fold_kernel,
        out_shape=jax.ShapeDtypeStruct((parts, *shares.shape[1:]), shares.dtype),
        compiler_params=params(),
        cost_estimate=pl.CostEstimate(flops=flops, bytes_accessed=4096, transcendentals=0),
        name="fold",
    )(shares)


def body(
    hidden_rows,
    chosen_query_rows,
    key_rows,
    chosen_value_rows,
    output_gradient,
    positions,
    counts,
    router,
):
    rows, width = chosen_query_rows.shape[1:]
    payload = pl.pallas_call(
        pack_kernel,
        out_shape=jax.ShapeDtypeStruct((Y, rows, 2 * KV_WIDTH + 128), jnp.bfloat16),
        in_specs=[HBM, HBM, HBM],
        out_specs=HBM,
        scratch_shapes=[
            pltpu.VMEM((1, rows), jnp.int32),
            pltpu.VMEM((rows, 2 * KV_WIDTH + 128), jnp.bfloat16),
            pltpu.SemaphoreType.DMA((3,)),
            pltpu.SemaphoreType.DMA((Y,)),
        ],
        compiler_params=params(FULL_VMEM),
        name="pack",
    )(key_rows, chosen_value_rows, positions)
    gathered = lax.all_to_all(payload, "ctx", 0, 0, tiled=True)

    gate, slope = pl.pallas_call(
        gate_kernel,
        out_shape=[jax.ShapeDtypeStruct((rows, 128), jnp.float32)] * 2,
        in_specs=[
            pl.BlockSpec(memory_space=pltpu.VMEM),
            pl.BlockSpec(memory_space=pltpu.VMEM),
            pl.BlockSpec(memory_space=pltpu.SMEM),
        ],
        compiler_params=params(FULL_VMEM),
        cost_estimate=pl.CostEstimate(
            flops=2 * rows * width, bytes_accessed=2 * rows * width, transcendentals=rows
        ),
        name="gate",
    )(hidden_rows, router.reshape(1, width), counts)

    query_places = jnp.tile(positions, (1, GROUP))
    heads = 2
    steps = KEY_VALUE_HEADS // heads
    span = heads * HEAD_SIZE
    wide_block = pl.BlockSpec((1, rows, heads * GROUP * HEAD_SIZE), lambda i: (0, 0, i))
    key_block = pl.BlockSpec((Y, rows, span), lambda i: (0, 0, i))
    value_block = pl.BlockSpec((Y, rows, span), lambda i: (0, 0, i + steps))
    place_block = pl.BlockSpec((Y, rows, 128), lambda i: (0, 0, 2 * KEY_VALUE_HEADS))

    def whole(*shape):
        return pl.BlockSpec(shape, lambda i: (0,) * len(shape))

    along = pl.pallas_call(
        forward_kernel,
        out_shape=jax.ShapeDtypeStruct((rows, 128), jnp.float32),
        compiler_params=params(),
        cost_estimate=pl.CostEstimate(
            flops=4 * rows * width * Y * rows,
            bytes_accessed=6 * rows * width,
            transcendentals=rows * QUERY_HEADS * Y * rows,
        ),
        name="forward",
    )(chosen_query_rows, output_gradient, gathered, query_places)
    chunk = width // PLANE
    term = pl.pallas_call(
        router_kernel,
        out_shape=jax.ShapeDtypeStruct((PLANE, 1, chunk), jnp.float32),
        compiler_params=params(),
        cost_estimate=pl.CostEstimate(
            flops=2 * rows * width, bytes_accessed=2 * rows * width, transcendentals=0
        ),
        name="router",
    )(along, slope, hidden_rows)

    query_gradient, *terms = pl.pallas_call(
        functools.partial(backward_kernel, heads),
        grid=(steps,),
        out_shape=[
            jax.ShapeDtypeStruct((1, rows, width), jnp.bfloat16),
            *[jax.ShapeDtypeStruct((rows, 2 * KV_WIDTH), jnp.bfloat16)] * Y,
        ],
        in_specs=[
            wide_block,
            wide_block,
            key_block,
            value_block,
            place_block,
            whole(1, GROUP * rows),
            whole(rows, 128),
        ],
        out_specs=[wide_block] + [pl.BlockSpec((rows, 2 * span), lambda i: (0, i))] * Y,
        compiler_params=params(FULL_VMEM),
        cost_estimate=pl.CostEstimate(
            flops=10 * rows * width * Y * rows,
            bytes_accessed=6 * rows * width,
            transcendentals=rows * QUERY_HEADS * Y * rows,
        ),
        name="backward",
    )(
        chosen_query_rows,
        output_gradient,
        gathered,
        gathered,
        gathered,
        query_places,
        gate,
    )

    plane = ("x", "core", "ctx")
    shares = lax.all_to_all(term, plane, 0, 0, tiled=True)
    share = fold(shares, Z, 8192)
    share, *terms = lax.optimization_barrier((share, *terms))
    lines = lax.all_to_all(share, "z", 0, 0, tiled=True)
    term_shares = [terms[0]] + [
        lax.ppermute(terms[back], "ctx", [(i, (i - back) % Y) for i in range(Y)])
        for back in range(1, Y)
    ]
    line = fold(lines, PLANE, FOLD_FLOPS)
    router_grad = lax.all_to_all(line, plane, 0, 0, tiled=True).reshape(width)
    key_gradient, value_gradient = pl.pallas_call(
        functools.partial(combine_kernel, span),
        out_shape=[jax.ShapeDtypeStruct((1, rows, KV_WIDTH), jnp.bfloat16)] * 2,
        compiler_params=params(),
        cost_estimate=pl.CostEstimate(
            flops=4 * rows * KV_WIDTH, bytes_accessed=20 * rows * KV_WIDTH, transcendentals=0
        ),
        name="combine",
    )(*term_shares)
    return query_gradient, key_gradient, value_gradient, router_grad


def solution(mesh):
    fine = Mesh(mesh.devices.reshape(X, Z, CORES, Y), ("x", "z", "core", "ctx"))
    seq = ("x", "z", "core")
    rows3 = P(seq, "ctx", None)
    rows2 = P(seq, "ctx")
    return jax.shard_map(
        body,
        mesh=fine,
        in_specs=(rows3, rows3, rows3, rows3, rows3, rows2, rows2, P()),
        out_specs=(rows3, rows3, rows3, P()),
        check_vma=False,
    )
```

```python
import functools
import math

import jax
import jax.numpy as jnp
from jax import lax
from jax.experimental import pallas as pl
from jax.experimental.pallas import tpu as pltpu
from jax.sharding import Mesh, PartitionSpec as P

QUERY_HEADS = 64
KEY_VALUE_HEADS = 8
HEAD_SIZE = 128
GROUP = QUERY_HEADS // KEY_VALUE_HEADS
KV_WIDTH = KEY_VALUE_HEADS * HEAD_SIZE
SCALE = 1.0 / math.sqrt(HEAD_SIZE)
LOG2_SCALE = SCALE * math.log2(math.e)
X, Z, CORES, Y = 4, 16, 2, 4
PLANE = X * CORES * Y
Y_FIRST, Z_FIRST, PLANE_FIRST = 0, 10, 17
VMEM_LIMIT = 48 * 1024 * 1024
FULL_VMEM = 60 * 1024 * 1024
FORWARD_VMEM = 50 * 1024 * 1024
FOLD_FLOPS = 1 << 35
HBM = pl.BlockSpec(memory_space=pltpu.HBM)
NT = (((1,), (1,)), ((), ()))
TN = (((0,), (0,)), ((), ()))
NN = (((1,), (0,)), ((), ()))


def dot(a, b, dims):
    return lax.dot_general(a, b, dims, preferred_element_type=jnp.float32)


def exchange(parts, axis, first):
    size = parts.shape[0]
    order = [(i + first) % size for i in range(size)]
    return lax.all_to_all(parts, axis, 0, 0, axis_index_groups=[order], tiled=True)


def params(limit=VMEM_LIMIT):
    return pltpu.CompilerParams(vmem_limit_bytes=limit)


def column(row, rows):
    wide = jnp.broadcast_to(row, (rows, rows))
    diagonal = lax.broadcasted_iota(jnp.int32, (rows, rows), 0) == lax.broadcasted_iota(
        jnp.int32, (rows, rows), 1
    )
    return jnp.sum(jnp.where(diagonal, wide.astype(jnp.float32), 0.0), axis=1, keepdims=True)


def pack_kernel(key_ref, value_ref, place_ref, out_ref, row_ref, block_ref, in_sems, out_sems):
    rows = key_ref.shape[1]
    fetches = [
        pltpu.make_async_copy(place_ref, row_ref, in_sems.at[0]),
        pltpu.make_async_copy(key_ref.at[0], block_ref.at[:, :KV_WIDTH], in_sems.at[1]),
        pltpu.make_async_copy(
            value_ref.at[0], block_ref.at[:, KV_WIDTH : 2 * KV_WIDTH], in_sems.at[2]
        ),
    ]
    for fetch in fetches:
        fetch.start()
    fetches[0].wait()
    places = column(row_ref[...], rows)
    high = jnp.floor(places * (1.0 / 16.0))
    low = places - 16.0 * high
    lane = lax.broadcasted_iota(jnp.int32, (rows, 128), 1)
    coded = jnp.where(lane == 0, high, jnp.where(lane == 1, low, 0.0))
    block_ref[:, 2 * KV_WIDTH :] = coded.astype(jnp.bfloat16)
    fetches[1].wait()
    fetches[2].wait()
    copies = [
        pltpu.make_async_copy(block_ref, out_ref.at[part], out_sems.at[part]) for part in range(Y)
    ]
    for copy in copies:
        copy.start()
    for copy in copies:
        copy.wait()


def gate_kernel(hidden_ref, router_ref, count_ref, gate_ref, slope_ref):
    rows, width = hidden_ref.shape[1:]
    step = 1024
    total = jnp.zeros((rows, 128), jnp.float32)
    for start in range(0, width, step):
        product = hidden_ref[0, :, start : start + step].astype(jnp.float32) * router_ref[
            :, start : start + step
        ]
        for piece in range(0, step, 128):
            total = total + product[:, piece : piece + 128]
    logits = jnp.sum(total, axis=1, keepdims=True)
    sigma = jax.nn.sigmoid(logits)
    slot = lax.broadcasted_iota(jnp.int32, (rows, 1), 0)
    valid = (slot < count_ref[0, 0]).astype(jnp.float32)
    gate_ref[...] = jnp.broadcast_to(sigma * valid, (rows, 128))
    slope_ref[...] = jnp.broadcast_to(sigma * (1.0 - sigma) * valid, (rows, 128))


def key_places(place_block):
    coded = place_block.reshape(-1, 128).astype(jnp.float32)
    return coded[:, 0:1] * 16.0 + coded[:, 1:2]


def stack_heads(block, first, rows):
    return jnp.concatenate(
        [block[:, (first + g) * HEAD_SIZE : (first + g + 1) * HEAD_SIZE] for g in range(GROUP)],
        axis=0,
    )


def mask_bias(places, query_places):
    return jnp.where(places <= query_places.astype(jnp.float32), 0.0, -1e30)


def weights_of(scores, bias):
    scores = scores + jnp.concatenate([bias] * (scores.shape[1] // bias.shape[1]), axis=1)
    top = jnp.max(scores, axis=0, keepdims=True)
    weights = jnp.exp2((scores - top) * LOG2_SCALE)
    return weights, jnp.sum(weights, axis=0, keepdims=True)


def forward_kernel(q_ref, grad_ref, pay_ref, qp_ref, slope_ref, hidden_ref, out_ref):
    rows = q_ref.shape[1]
    bias = mask_bias(key_places(pay_ref[:, :, 2 * KV_WIDTH :]), qp_ref[:, : 2 * rows])

    def products(c):
        left = c * HEAD_SIZE
        queries = stack_heads(q_ref[0], c * GROUP, rows)
        grads = stack_heads(grad_ref[0], c * GROUP, rows)
        keys = pay_ref[:, :, left : left + HEAD_SIZE].reshape(-1, HEAD_SIZE)
        left = left + KV_WIDTH
        values = pay_ref[:, :, left : left + HEAD_SIZE].reshape(-1, HEAD_SIZE)
        return dot(keys, queries, NT), dot(values, grads, NT)

    acc = jnp.zeros((1, GROUP * rows), jnp.float32)
    for c in range(KEY_VALUE_HEADS):
        scores, along = products(c)
        weights, total = weights_of(scores, bias)
        acc = acc + jnp.sum(weights * along, axis=0, keepdims=True) / total
    row_sum = acc[:, :rows]
    for g in range(1, GROUP):
        row_sum = row_sum + acc[:, g * rows : (g + 1) * rows]
    wide = jnp.broadcast_to(row_sum, (rows, rows))
    diagonal = lax.broadcasted_iota(jnp.int32, (rows, rows), 0) == lax.broadcasted_iota(
        jnp.int32, (rows, rows), 1
    )
    down = jnp.sum(jnp.where(diagonal, wide, 0.0), axis=1, keepdims=True)
    logit_grad = down * slope_ref[...] * (1.0 / math.sqrt(X * Z * CORES * Y * rows))
    chunk = out_ref.shape[2]
    for part in range(PLANE):
        for lane in range(0, chunk, 128):
            left = part * chunk + lane
            block = hidden_ref[0, :, left : left + 128].astype(jnp.float32)
            out_ref[part, :, lane : lane + 128] = jnp.sum(
                block * logit_grad, axis=0, keepdims=True
            )


def backward_kernel(
    heads,
    q_ref,
    grad_ref,
    k_ref,
    v_ref,
    kp_ref,
    qp_ref,
    gate_ref,
    dq_ref,
    *term_refs,
):
    rows = q_ref.shape[1]
    me = lax.axis_index("ctx")
    owners = [lax.rem(me + 2 * Y - back - Y_FIRST, Y) for back in range(Y)]

    def blocks(ref, columns):
        return jnp.concatenate([ref[owner, :, columns] for owner in owners], axis=0)

    bias = mask_bias(key_places(blocks(kp_ref, slice(0, 128))), qp_ref[:, : 2 * rows])
    gate = gate_ref[:, :1]
    for c in range(heads):
        queries = stack_heads(q_ref[0], c * GROUP, rows)
        grads = jnp.concatenate(
            [
                (
                    grad_ref[
                        0, :, (c * GROUP + g) * HEAD_SIZE : (c * GROUP + g + 1) * HEAD_SIZE
                    ].astype(jnp.float32)
                    * gate
                ).astype(jnp.bfloat16)
                for g in range(GROUP)
            ],
            axis=0,
        )
        own = slice(c * HEAD_SIZE, (c + 1) * HEAD_SIZE)
        beside = slice((heads + c) * HEAD_SIZE, (heads + c + 1) * HEAD_SIZE)
        keys = blocks(k_ref, own)
        values = blocks(v_ref, own)
        weights, total = weights_of(dot(keys, queries, NT), bias)
        probs = (weights * (1.0 / total)).astype(jnp.bfloat16)
        probs32 = probs.astype(jnp.float32)
        grad_probs = dot(values, grads, NT)
        row_dot = jnp.sum(probs32 * grad_probs, axis=0, keepdims=True)
        grad_scores = (probs32 * (grad_probs - row_dot)).astype(jnp.bfloat16)
        dv = dot(probs, grads, NN).astype(jnp.bfloat16)
        dk = (dot(grad_scores, queries, NN) * SCALE).astype(jnp.bfloat16)
        dq = (dot(grad_scores, keys, TN) * SCALE).astype(jnp.bfloat16)
        for back, term_ref in enumerate(term_refs):
            term_ref[:, own] = dk[back * rows : (back + 1) * rows]
            term_ref[:, beside] = dv[back * rows : (back + 1) * rows]
        for g in range(GROUP):
            left = (c * GROUP + g) * HEAD_SIZE
            dq_ref[0, :, left : left + HEAD_SIZE] = dq[g * rows : (g + 1) * rows]


def combine_kernel(span, *refs):
    share_refs, (dk_ref, dv_ref) = refs[:-2], refs[-2:]
    total = share_refs[0][...].astype(jnp.float32)
    for share_ref in share_refs[1:]:
        total = total + share_ref[...].astype(jnp.float32)
    total = total.astype(jnp.bfloat16)
    for i in range(KV_WIDTH // span):
        own = slice(i * span, (i + 1) * span)
        dk_ref[0, :, own] = total[:, 2 * i * span : (2 * i + 1) * span]
        dv_ref[0, :, own] = total[:, (2 * i + 1) * span : (2 * i + 2) * span]


def fold_kernel(share_ref, out_ref):
    total = share_ref[0]
    for part in range(1, share_ref.shape[0]):
        total = total + share_ref[part]
    for part in range(out_ref.shape[0]):
        out_ref[part] = total


def fold(shares, parts, flops):
    return pl.pallas_call(
        fold_kernel,
        out_shape=jax.ShapeDtypeStruct((parts, *shares.shape[1:]), shares.dtype),
        compiler_params=params(),
        cost_estimate=pl.CostEstimate(flops=flops, bytes_accessed=4096, transcendentals=0),
        name="fold",
    )(shares)


def body(
    hidden_rows,
    chosen_query_rows,
    key_rows,
    chosen_value_rows,
    output_gradient,
    positions,
    counts,
    router,
):
    rows, width = chosen_query_rows.shape[1:]
    payload = pl.pallas_call(
        pack_kernel,
        out_shape=jax.ShapeDtypeStruct((Y, rows, 2 * KV_WIDTH + 128), jnp.bfloat16),
        in_specs=[HBM, HBM, HBM],
        out_specs=HBM,
        scratch_shapes=[
            pltpu.VMEM((1, rows), jnp.int32),
            pltpu.VMEM((rows, 2 * KV_WIDTH + 128), jnp.bfloat16),
            pltpu.SemaphoreType.DMA((3,)),
            pltpu.SemaphoreType.DMA((Y,)),
        ],
        compiler_params=params(FULL_VMEM),
        name="pack",
    )(key_rows, chosen_value_rows, positions)
    gathered = exchange(payload, "ctx", Y_FIRST)

    gate, slope = pl.pallas_call(
        gate_kernel,
        out_shape=[jax.ShapeDtypeStruct((rows, 128), jnp.float32)] * 2,
        in_specs=[
            pl.BlockSpec(memory_space=pltpu.VMEM),
            pl.BlockSpec(memory_space=pltpu.VMEM),
            pl.BlockSpec(memory_space=pltpu.SMEM),
        ],
        compiler_params=params(FORWARD_VMEM),
        cost_estimate=pl.CostEstimate(
            flops=2 * rows * width, bytes_accessed=2 * rows * width, transcendentals=rows
        ),
        name="gate",
    )(hidden_rows, router.reshape(1, width), counts)

    query_places = jnp.tile(positions, (1, GROUP))
    heads = 2
    steps = KEY_VALUE_HEADS // heads
    span = heads * HEAD_SIZE
    wide_block = pl.BlockSpec((1, rows, heads * GROUP * HEAD_SIZE), lambda i: (0, 0, i))
    key_block = pl.BlockSpec((Y, rows, span), lambda i: (0, 0, i))
    value_block = pl.BlockSpec((Y, rows, span), lambda i: (0, 0, i + steps))
    place_block = pl.BlockSpec((Y, rows, 128), lambda i: (0, 0, 2 * KEY_VALUE_HEADS))

    def whole(*shape):
        return pl.BlockSpec(shape, lambda i: (0,) * len(shape))

    chunk = width // PLANE
    term = pl.pallas_call(
        forward_kernel,
        out_shape=jax.ShapeDtypeStruct((PLANE, 1, chunk), jnp.float32),
        compiler_params=params(FORWARD_VMEM),
        cost_estimate=pl.CostEstimate(
            flops=4 * rows * width * Y * rows,
            bytes_accessed=6 * rows * width,
            transcendentals=rows * QUERY_HEADS * Y * rows,
        ),
        name="forward",
    )(chosen_query_rows, output_gradient, gathered, query_places, slope, hidden_rows)

    query_gradient, *terms = pl.pallas_call(
        functools.partial(backward_kernel, heads),
        grid=(steps,),
        out_shape=[
            jax.ShapeDtypeStruct((1, rows, width), jnp.bfloat16),
            *[jax.ShapeDtypeStruct((rows, 2 * KV_WIDTH), jnp.bfloat16)] * Y,
        ],
        in_specs=[
            wide_block,
            wide_block,
            key_block,
            value_block,
            place_block,
            whole(1, GROUP * rows),
            whole(rows, 128),
        ],
        out_specs=[wide_block] + [pl.BlockSpec((rows, 2 * span), lambda i: (0, i))] * Y,
        compiler_params=params(FULL_VMEM),
        cost_estimate=pl.CostEstimate(
            flops=10 * rows * width * Y * rows,
            bytes_accessed=6 * rows * width,
            transcendentals=rows * QUERY_HEADS * Y * rows,
        ),
        name="backward",
    )(
        chosen_query_rows,
        output_gradient,
        gathered,
        gathered,
        gathered,
        query_places,
        gate,
    )

    plane = ("x", "core", "ctx")
    shares = exchange(term, plane, PLANE_FIRST)
    share = fold(shares, Z, 8192)
    share, *terms = lax.optimization_barrier((share, *terms))
    lines = exchange(share, "z", Z_FIRST)
    term_shares = [terms[0]] + [
        lax.ppermute(terms[back], "ctx", [(i, (i - back) % Y) for i in range(Y)])
        for back in range(1, Y)
    ]
    line = fold(lines, PLANE, FOLD_FLOPS)
    router_grad = exchange(line, plane, PLANE_FIRST).reshape(width)
    key_gradient, value_gradient = pl.pallas_call(
        functools.partial(combine_kernel, span),
        out_shape=[jax.ShapeDtypeStruct((1, rows, KV_WIDTH), jnp.bfloat16)] * 2,
        compiler_params=params(),
        cost_estimate=pl.CostEstimate(
            flops=4 * rows * KV_WIDTH, bytes_accessed=20 * rows * KV_WIDTH, transcendentals=0
        ),
        name="combine",
    )(*term_shares)
    router_grad, key_gradient = lax.optimization_barrier((router_grad, key_gradient))
    return query_gradient, key_gradient, value_gradient, router_grad


def solution(mesh):
    fine = Mesh(mesh.devices.reshape(X, Z, CORES, Y), ("x", "z", "core", "ctx"))
    seq = ("x", "z", "core")
    rows3 = P(seq, "ctx", None)
    rows2 = P(seq, "ctx")
    return jax.shard_map(
        body,
        mesh=fine,
        in_specs=(rows3, rows3, rows3, rows3, rows3, rows2, rows2, P()),
        out_specs=(rows3, rows3, rows3, P()),
        check_vma=False,
    )
```

```python
import functools
import math

import jax
import jax.numpy as jnp
from jax import lax
from jax.experimental import pallas as pl
from jax.experimental.pallas import tpu as pltpu
from jax.sharding import Mesh, PartitionSpec as P

QUERY_HEADS = 64
KEY_VALUE_HEADS = 8
HEAD_SIZE = 128
GROUP = QUERY_HEADS // KEY_VALUE_HEADS
KV_WIDTH = KEY_VALUE_HEADS * HEAD_SIZE
SCALE = 1.0 / math.sqrt(HEAD_SIZE)
LOG2_SCALE = SCALE * math.log2(math.e)
X, Z, CORES, Y = 4, 16, 2, 4
PLANE = X * CORES * Y
Y_FIRST, Z_FIRST, PLANE_FIRST = 0, 10, 17
VMEM_LIMIT = 48 * 1024 * 1024
FULL_VMEM = 60 * 1024 * 1024
FOLD_FLOPS = 1 << 35
HBM = pl.BlockSpec(memory_space=pltpu.HBM)
NT = (((1,), (1,)), ((), ()))
TN = (((0,), (0,)), ((), ()))
NN = (((1,), (0,)), ((), ()))


def dot(a, b, dims):
    return lax.dot_general(a, b, dims, preferred_element_type=jnp.float32)


def exchange(parts, axis, first):
    size = parts.shape[0]
    order = [(i + first) % size for i in range(size)]
    return lax.all_to_all(parts, axis, 0, 0, axis_index_groups=[order], tiled=True)


def params(limit=VMEM_LIMIT):
    return pltpu.CompilerParams(vmem_limit_bytes=limit)


def column(row, rows):
    wide = jnp.broadcast_to(row, (rows, rows))
    diagonal = lax.broadcasted_iota(jnp.int32, (rows, rows), 0) == lax.broadcasted_iota(
        jnp.int32, (rows, rows), 1
    )
    return jnp.sum(jnp.where(diagonal, wide.astype(jnp.float32), 0.0), axis=1, keepdims=True)


def pack_kernel(key_ref, value_ref, place_ref, out_ref, row_ref, block_ref, in_sems, out_sems):
    rows = key_ref.shape[1]
    fetches = [
        pltpu.make_async_copy(place_ref, row_ref, in_sems.at[0]),
        pltpu.make_async_copy(key_ref.at[0], block_ref.at[:, :KV_WIDTH], in_sems.at[1]),
        pltpu.make_async_copy(
            value_ref.at[0], block_ref.at[:, KV_WIDTH : 2 * KV_WIDTH], in_sems.at[2]
        ),
    ]
    for fetch in fetches:
        fetch.start()
    fetches[0].wait()
    places = column(row_ref[...], rows)
    high = jnp.floor(places * (1.0 / 16.0))
    low = places - 16.0 * high
    lane = lax.broadcasted_iota(jnp.int32, (rows, 128), 1)
    coded = jnp.where(lane == 0, high, jnp.where(lane == 1, low, 0.0))
    block_ref[:, 2 * KV_WIDTH :] = coded.astype(jnp.bfloat16)
    fetches[1].wait()
    fetches[2].wait()
    copies = [
        pltpu.make_async_copy(block_ref, out_ref.at[part], out_sems.at[part]) for part in range(Y)
    ]
    for copy in copies:
        copy.start()
    for copy in copies:
        copy.wait()


def key_places(place_block):
    coded = place_block.reshape(-1, 128).astype(jnp.float32)
    return coded[:, 0:1] * 16.0 + coded[:, 1:2]


def stack_heads(block, first, rows):
    return jnp.concatenate(
        [block[:, (first + g) * HEAD_SIZE : (first + g + 1) * HEAD_SIZE] for g in range(GROUP)],
        axis=0,
    )


def mask_bias(places, query_places):
    return jnp.where(places <= query_places.astype(jnp.float32), 0.0, -1e30)


def weights_of(scores, bias):
    scores = scores + jnp.concatenate([bias] * (scores.shape[1] // bias.shape[1]), axis=1)
    top = jnp.max(scores, axis=0, keepdims=True)
    weights = jnp.exp2((scores - top) * LOG2_SCALE)
    return weights, jnp.sum(weights, axis=0, keepdims=True)


def forward_kernel(q_ref, grad_ref, pay_ref, qp_ref, out_ref):
    rows = q_ref.shape[1]
    bias = mask_bias(key_places(pay_ref[:, :, 2 * KV_WIDTH :]), qp_ref[:, : 2 * rows])

    acc = jnp.zeros((1, GROUP * rows), jnp.float32)
    for c in range(KEY_VALUE_HEADS):
        left = c * HEAD_SIZE
        queries = stack_heads(q_ref[0], c * GROUP, rows)
        keys = pay_ref[:, :, left : left + HEAD_SIZE].reshape(-1, HEAD_SIZE)
        weights, total = weights_of(dot(keys, queries, NT), bias)
        left = left + KV_WIDTH
        grads = stack_heads(grad_ref[0], c * GROUP, rows)
        values = pay_ref[:, :, left : left + HEAD_SIZE].reshape(-1, HEAD_SIZE)
        along = dot(values, grads, NT)
        acc = acc + jnp.sum(weights * along, axis=0, keepdims=True) / total
    row_sum = acc[:, :rows]
    for g in range(1, GROUP):
        row_sum = row_sum + acc[:, g * rows : (g + 1) * rows]
    wide = jnp.broadcast_to(row_sum, (rows, rows))
    diagonal = lax.broadcasted_iota(jnp.int32, (rows, rows), 0) == lax.broadcasted_iota(
        jnp.int32, (rows, rows), 1
    )
    down = jnp.sum(jnp.where(diagonal, wide, 0.0), axis=1, keepdims=True)
    out_ref[...] = jnp.broadcast_to(down, (rows, 128))


def router_kernel(along_ref, hidden_ref, router_ref, count_ref, out_ref, gate_ref):
    rows, width = hidden_ref.shape[1:]
    total = jnp.zeros((rows, 128), jnp.float32)
    for left in range(0, width, 128):
        block = hidden_ref[0, :, left : left + 128].astype(jnp.float32)
        total = total + block * router_ref[:, left : left + 128]
    sigma = jax.nn.sigmoid(jnp.sum(total, axis=1, keepdims=True))
    slot = lax.broadcasted_iota(jnp.int32, (rows, 1), 0)
    valid = (slot < count_ref[0, 0]).astype(jnp.float32)
    gate_ref[...] = jnp.broadcast_to(sigma * valid, (rows, 128))
    slope = sigma * (1.0 - sigma) * valid
    logit_grad = along_ref[...] * slope * (1.0 / math.sqrt(X * Z * CORES * Y * rows))
    chunk = out_ref.shape[2]
    for part in range(PLANE):
        for lane in range(0, chunk, 128):
            left = part * chunk + lane
            block = hidden_ref[0, :, left : left + 128].astype(jnp.float32)
            out_ref[part, :, lane : lane + 128] = jnp.sum(
                block * logit_grad, axis=0, keepdims=True
            )


def backward_kernel(
    heads,
    q_ref,
    grad_ref,
    k_ref,
    v_ref,
    kp_ref,
    qp_ref,
    gate_ref,
    dq_ref,
    *term_refs,
):
    rows = q_ref.shape[1]
    me = lax.axis_index("ctx")
    owners = [lax.rem(me + 2 * Y - back - Y_FIRST, Y) for back in range(Y)]

    def blocks(ref, columns):
        return jnp.concatenate([ref[owner, :, columns] for owner in owners], axis=0)

    bias = mask_bias(key_places(blocks(kp_ref, slice(0, 128))), qp_ref[:, : 2 * rows])
    gate = gate_ref[:, :1]
    for c in range(heads):
        queries = stack_heads(q_ref[0], c * GROUP, rows)
        grads = jnp.concatenate(
            [
                (
                    grad_ref[
                        0, :, (c * GROUP + g) * HEAD_SIZE : (c * GROUP + g + 1) * HEAD_SIZE
                    ].astype(jnp.float32)
                    * gate
                ).astype(jnp.bfloat16)
                for g in range(GROUP)
            ],
            axis=0,
        )
        own = slice(c * HEAD_SIZE, (c + 1) * HEAD_SIZE)
        beside = slice((heads + c) * HEAD_SIZE, (heads + c + 1) * HEAD_SIZE)
        keys = blocks(k_ref, own)
        values = blocks(v_ref, own)
        weights, total = weights_of(dot(keys, queries, NT), bias)
        probs = (weights * (1.0 / total)).astype(jnp.bfloat16)
        probs32 = probs.astype(jnp.float32)
        grad_probs = dot(values, grads, NT)
        row_dot = jnp.sum(probs32 * grad_probs, axis=0, keepdims=True)
        grad_scores = (probs32 * (grad_probs - row_dot)).astype(jnp.bfloat16)
        dv = dot(probs, grads, NN).astype(jnp.bfloat16)
        dk = (dot(grad_scores, queries, NN) * SCALE).astype(jnp.bfloat16)
        dq = (dot(grad_scores, keys, TN) * SCALE).astype(jnp.bfloat16)
        for back, term_ref in enumerate(term_refs):
            term_ref[:, own] = dk[back * rows : (back + 1) * rows]
            term_ref[:, beside] = dv[back * rows : (back + 1) * rows]
        for g in range(GROUP):
            left = (c * GROUP + g) * HEAD_SIZE
            dq_ref[0, :, left : left + HEAD_SIZE] = dq[g * rows : (g + 1) * rows]


def combine_kernel(span, *refs):
    share_refs, (dk_ref, dv_ref) = refs[:-2], refs[-2:]
    total = share_refs[0][...].astype(jnp.float32)
    for share_ref in share_refs[1:]:
        total = total + share_ref[...].astype(jnp.float32)
    total = total.astype(jnp.bfloat16)
    for i in range(KV_WIDTH // span):
        own = slice(i * span, (i + 1) * span)
        dk_ref[0, :, own] = total[:, 2 * i * span : (2 * i + 1) * span]
        dv_ref[0, :, own] = total[:, (2 * i + 1) * span : (2 * i + 2) * span]


def fold_kernel(share_ref, out_ref):
    total = share_ref[0]
    for part in range(1, share_ref.shape[0]):
        total = total + share_ref[part]
    for part in range(out_ref.shape[0]):
        out_ref[part] = total


def fold(shares, parts, flops):
    return pl.pallas_call(
        fold_kernel,
        out_shape=jax.ShapeDtypeStruct((parts, *shares.shape[1:]), shares.dtype),
        compiler_params=params(),
        cost_estimate=pl.CostEstimate(flops=flops, bytes_accessed=4096, transcendentals=0),
        name="fold",
    )(shares)


def body(
    hidden_rows,
    chosen_query_rows,
    key_rows,
    chosen_value_rows,
    output_gradient,
    positions,
    counts,
    router,
):
    rows, width = chosen_query_rows.shape[1:]
    payload = pl.pallas_call(
        pack_kernel,
        out_shape=jax.ShapeDtypeStruct((Y, rows, 2 * KV_WIDTH + 128), jnp.bfloat16),
        in_specs=[HBM, HBM, HBM],
        out_specs=HBM,
        scratch_shapes=[
            pltpu.VMEM((1, rows), jnp.int32),
            pltpu.VMEM((rows, 2 * KV_WIDTH + 128), jnp.bfloat16),
            pltpu.SemaphoreType.DMA((3,)),
            pltpu.SemaphoreType.DMA((Y,)),
        ],
        compiler_params=params(FULL_VMEM),
        name="pack",
    )(key_rows, chosen_value_rows, positions)
    gathered = exchange(payload, "ctx", Y_FIRST)

    query_places = jnp.tile(positions, (1, GROUP))
    heads = 2
    steps = KEY_VALUE_HEADS // heads
    span = heads * HEAD_SIZE
    wide_block = pl.BlockSpec((1, rows, heads * GROUP * HEAD_SIZE), lambda i: (0, 0, i))
    key_block = pl.BlockSpec((Y, rows, span), lambda i: (0, 0, i))
    value_block = pl.BlockSpec((Y, rows, span), lambda i: (0, 0, i + steps))
    place_block = pl.BlockSpec((Y, rows, 128), lambda i: (0, 0, 2 * KEY_VALUE_HEADS))

    def whole(*shape):
        return pl.BlockSpec(shape, lambda i: (0,) * len(shape))

    along = pl.pallas_call(
        forward_kernel,
        out_shape=jax.ShapeDtypeStruct((rows, 128), jnp.float32),
        compiler_params=params(),
        cost_estimate=pl.CostEstimate(
            flops=4 * rows * width * Y * rows,
            bytes_accessed=6 * rows * width,
            transcendentals=rows * QUERY_HEADS * Y * rows,
        ),
        name="forward",
    )(chosen_query_rows, output_gradient, gathered, query_places)
    chunk = width // PLANE
    vmem = pl.BlockSpec(memory_space=pltpu.VMEM)
    term, gate = pl.pallas_call(
        router_kernel,
        out_shape=[
            jax.ShapeDtypeStruct((PLANE, 1, chunk), jnp.float32),
            jax.ShapeDtypeStruct((rows, 128), jnp.float32),
        ],
        in_specs=[vmem, vmem, vmem, pl.BlockSpec(memory_space=pltpu.SMEM)],
        compiler_params=params(),
        cost_estimate=pl.CostEstimate(
            flops=4 * rows * width, bytes_accessed=2 * rows * width, transcendentals=rows
        ),
        name="router",
    )(along, hidden_rows, router.reshape(1, width), counts)

    query_gradient, *terms = pl.pallas_call(
        functools.partial(backward_kernel, heads),
        grid=(steps,),
        out_shape=[
            jax.ShapeDtypeStruct((1, rows, width), jnp.bfloat16),
            *[jax.ShapeDtypeStruct((rows, 2 * KV_WIDTH), jnp.bfloat16)] * Y,
        ],
        in_specs=[
            wide_block,
            wide_block,
            key_block,
            value_block,
            place_block,
            whole(1, GROUP * rows),
            whole(rows, 128),
        ],
        out_specs=[wide_block] + [pl.BlockSpec((rows, 2 * span), lambda i: (0, i))] * Y,
        compiler_params=params(FULL_VMEM),
        cost_estimate=pl.CostEstimate(
            flops=10 * rows * width * Y * rows,
            bytes_accessed=6 * rows * width,
            transcendentals=rows * QUERY_HEADS * Y * rows,
        ),
        name="backward",
    )(
        chosen_query_rows,
        output_gradient,
        gathered,
        gathered,
        gathered,
        query_places,
        gate,
    )

    plane = ("x", "core", "ctx")
    shares = exchange(term, plane, PLANE_FIRST)
    share = fold(shares, Z, 8192)
    share, *terms = lax.optimization_barrier((share, *terms))
    lines = exchange(share, "z", Z_FIRST)
    term_shares = [terms[0]] + [
        lax.ppermute(terms[back], "ctx", [(i, i - back) for i in range(back, Y)])
        for back in range(1, Y)
    ]
    line = fold(lines, PLANE, FOLD_FLOPS)
    router_grad = exchange(line, plane, PLANE_FIRST).reshape(width)
    key_gradient, value_gradient = pl.pallas_call(
        functools.partial(combine_kernel, span),
        out_shape=[jax.ShapeDtypeStruct((1, rows, KV_WIDTH), jnp.bfloat16)] * 2,
        compiler_params=params(),
        cost_estimate=pl.CostEstimate(
            flops=4 * rows * KV_WIDTH, bytes_accessed=20 * rows * KV_WIDTH, transcendentals=0
        ),
        name="combine",
    )(*term_shares)
    router_grad, key_gradient = lax.optimization_barrier((router_grad, key_gradient))
    return query_gradient, key_gradient, value_gradient, router_grad


def solution(mesh):
    fine = Mesh(mesh.devices.reshape(X, Z, CORES, Y), ("x", "z", "core", "ctx"))
    seq = ("x", "z", "core")
    rows3 = P(seq, "ctx", None)
    rows2 = P(seq, "ctx")
    return jax.shard_map(
        body,
        mesh=fine,
        in_specs=(rows3, rows3, rows3, rows3, rows3, rows2, rows2, P()),
        out_specs=(rows3, rows3, rows3, P()),
        check_vma=False,
    )
```

```python
import functools
import math

import jax
import jax.numpy as jnp
from jax import lax
from jax.experimental import pallas as pl
from jax.experimental.pallas import tpu as pltpu
from jax.sharding import Mesh, PartitionSpec as P

QUERY_HEADS = 64
KEY_VALUE_HEADS = 8
HEAD_SIZE = 128
GROUP = QUERY_HEADS // KEY_VALUE_HEADS
KV_WIDTH = KEY_VALUE_HEADS * HEAD_SIZE
SCALE = 1.0 / math.sqrt(HEAD_SIZE)
LOG2_SCALE = SCALE * math.log2(math.e)
X, Z, CORES, Y = 4, 16, 2, 4
PLANE = X * CORES * Y
Y_FIRST, Z_FIRST, SUM_FIRST, SPREAD_FIRST = 0, 12, 17, 19
VMEM_LIMIT = 48 * 1024 * 1024
FULL_VMEM = 60 * 1024 * 1024
BACKWARD_VMEM = 53 * 1024 * 1024
FOLD_FLOPS = 1 << 35
HBM = pl.BlockSpec(memory_space=pltpu.HBM)
NT = (((1,), (1,)), ((), ()))
TN = (((0,), (0,)), ((), ()))
NN = (((1,), (0,)), ((), ()))


def dot(a, b, dims):
    return lax.dot_general(a, b, dims, preferred_element_type=jnp.float32)


def exchange(parts, axis, first):
    size = parts.shape[0]
    order = [(i + first) % size for i in range(size)]
    return lax.all_to_all(parts, axis, 0, 0, axis_index_groups=[order], tiled=True)


def params(limit=VMEM_LIMIT):
    return pltpu.CompilerParams(vmem_limit_bytes=limit)


def column(row, rows):
    wide = jnp.broadcast_to(row, (rows, rows))
    diagonal = lax.broadcasted_iota(jnp.int32, (rows, rows), 0) == lax.broadcasted_iota(
        jnp.int32, (rows, rows), 1
    )
    return jnp.sum(jnp.where(diagonal, wide.astype(jnp.float32), 0.0), axis=1, keepdims=True)


def pack_kernel(key_ref, value_ref, place_ref, out_ref, row_ref, block_ref, in_sems, out_sems):
    rows = key_ref.shape[1]
    fetches = [
        pltpu.make_async_copy(place_ref, row_ref, in_sems.at[0]),
        pltpu.make_async_copy(key_ref.at[0], block_ref.at[:, :KV_WIDTH], in_sems.at[1]),
        pltpu.make_async_copy(
            value_ref.at[0], block_ref.at[:, KV_WIDTH : 2 * KV_WIDTH], in_sems.at[2]
        ),
    ]
    for fetch in fetches:
        fetch.start()
    fetches[0].wait()
    places = column(row_ref[...], rows)
    high = jnp.floor(places * (1.0 / 16.0))
    low = places - 16.0 * high
    lane = lax.broadcasted_iota(jnp.int32, (rows, 128), 1)
    coded = jnp.where(lane == 0, high, jnp.where(lane == 1, low, 0.0))
    block_ref[:, 2 * KV_WIDTH :] = coded.astype(jnp.bfloat16)
    fetches[1].wait()
    fetches[2].wait()
    copies = [
        pltpu.make_async_copy(block_ref, out_ref.at[part], out_sems.at[part]) for part in range(Y)
    ]
    for copy in copies:
        copy.start()
    for copy in copies:
        copy.wait()


def key_places(place_block):
    coded = place_block.reshape(-1, 128).astype(jnp.float32)
    return coded[:, 0:1] * 16.0 + coded[:, 1:2]


def stack_heads(block, first, rows):
    return jnp.concatenate(
        [block[:, (first + g) * HEAD_SIZE : (first + g + 1) * HEAD_SIZE] for g in range(GROUP)],
        axis=0,
    )


def mask_bias(places, query_places):
    return jnp.where(places <= query_places.astype(jnp.float32), 0.0, -1e30)


def weights_of(scores, bias):
    scores = scores + jnp.concatenate([bias] * (scores.shape[1] // bias.shape[1]), axis=1)
    top = jnp.max(scores, axis=0, keepdims=True)
    weights = jnp.exp2((scores - top) * LOG2_SCALE)
    return weights, jnp.sum(weights, axis=0, keepdims=True)


def forward_kernel(q_ref, grad_ref, pay_ref, qp_ref, out_ref):
    rows = q_ref.shape[1]
    bias = mask_bias(key_places(pay_ref[:, :, 2 * KV_WIDTH :]), qp_ref[:, : 2 * rows])

    acc = jnp.zeros((1, GROUP * rows), jnp.float32)
    for c in range(KEY_VALUE_HEADS):
        left = c * HEAD_SIZE
        queries = stack_heads(q_ref[0], c * GROUP, rows)
        keys = pay_ref[:, :, left : left + HEAD_SIZE].reshape(-1, HEAD_SIZE)
        weights, total = weights_of(dot(keys, queries, NT), bias)
        left = left + KV_WIDTH
        grads = stack_heads(grad_ref[0], c * GROUP, rows)
        values = pay_ref[:, :, left : left + HEAD_SIZE].reshape(-1, HEAD_SIZE)
        along = dot(values, grads, NT)
        acc = acc + jnp.sum(weights * along, axis=0, keepdims=True) / total
    row_sum = acc[:, :rows]
    for g in range(1, GROUP):
        row_sum = row_sum + acc[:, g * rows : (g + 1) * rows]
    wide = jnp.broadcast_to(row_sum, (rows, rows))
    diagonal = lax.broadcasted_iota(jnp.int32, (rows, rows), 0) == lax.broadcasted_iota(
        jnp.int32, (rows, rows), 1
    )
    down = jnp.sum(jnp.where(diagonal, wide, 0.0), axis=1, keepdims=True)
    out_ref[...] = jnp.broadcast_to(down, (rows, 128))


def router_kernel(along_ref, hidden_ref, router_ref, count_ref, out_ref, gate_ref):
    rows, width = hidden_ref.shape[1:]
    total = jnp.zeros((rows, 128), jnp.float32)
    for left in range(0, width, 128):
        block = hidden_ref[0, :, left : left + 128].astype(jnp.float32)
        total = total + block * router_ref[:, left : left + 128]
    sigma = jax.nn.sigmoid(jnp.sum(total, axis=1, keepdims=True))
    slot = lax.broadcasted_iota(jnp.int32, (rows, 1), 0)
    valid = (slot < count_ref[0, 0]).astype(jnp.float32)
    gate_ref[...] = jnp.broadcast_to(sigma * valid, (rows, 128))
    slope = sigma * (1.0 - sigma) * valid
    logit_grad = along_ref[...] * slope * (1.0 / math.sqrt(X * Z * CORES * Y * rows))
    chunk = out_ref.shape[2]
    for part in range(PLANE):
        column = (part + SUM_FIRST - SPREAD_FIRST) % PLANE * chunk
        for lane in range(0, chunk, 128):
            left = column + lane
            block = hidden_ref[0, :, left : left + 128].astype(jnp.float32)
            out_ref[part, :, lane : lane + 128] = jnp.sum(
                block * logit_grad, axis=0, keepdims=True
            )


def backward_kernel(
    heads,
    q_ref,
    grad_ref,
    k_ref,
    v_ref,
    kp_ref,
    qp_ref,
    gate_ref,
    dq_ref,
    *term_refs,
):
    rows = q_ref.shape[1]
    me = lax.axis_index("ctx")
    owners = [lax.rem(me + 2 * Y - back - Y_FIRST, Y) for back in range(Y)]

    def blocks(ref, columns):
        return jnp.concatenate([ref[owner, :, columns] for owner in owners], axis=0)

    bias = mask_bias(key_places(blocks(kp_ref, slice(0, 128))), qp_ref[:, : 2 * rows])
    gate = gate_ref[:, :1]
    for c in range(heads):
        queries = stack_heads(q_ref[0], c * GROUP, rows)
        grads = jnp.concatenate(
            [
                (
                    grad_ref[
                        0, :, (c * GROUP + g) * HEAD_SIZE : (c * GROUP + g + 1) * HEAD_SIZE
                    ].astype(jnp.float32)
                    * gate
                ).astype(jnp.bfloat16)
                for g in range(GROUP)
            ],
            axis=0,
        )
        own = slice(c * HEAD_SIZE, (c + 1) * HEAD_SIZE)
        beside = slice((heads + c) * HEAD_SIZE, (heads + c + 1) * HEAD_SIZE)
        keys = blocks(k_ref, own)
        values = blocks(v_ref, own)
        weights, total = weights_of(dot(keys, queries, NT), bias)
        probs = (weights * (1.0 / total)).astype(jnp.bfloat16)
        probs32 = probs.astype(jnp.float32)
        grad_probs = dot(values, grads, NT)
        row_dot = jnp.sum(probs32 * grad_probs, axis=0, keepdims=True)
        grad_scores = (probs32 * (grad_probs - row_dot)).astype(jnp.bfloat16)
        dv = dot(probs, grads, NN).astype(jnp.bfloat16)
        dk = (dot(grad_scores, queries, NN) * SCALE).astype(jnp.bfloat16)
        dq = (dot(grad_scores, keys, TN) * SCALE).astype(jnp.bfloat16)
        for back, term_ref in enumerate(term_refs):
            term_ref[:, own] = dk[back * rows : (back + 1) * rows]
            term_ref[:, beside] = dv[back * rows : (back + 1) * rows]
        for g in range(GROUP):
            left = (c * GROUP + g) * HEAD_SIZE
            dq_ref[0, :, left : left + HEAD_SIZE] = dq[g * rows : (g + 1) * rows]


def combine_kernel(span, *refs):
    share_refs, (dk_ref, dv_ref) = refs[:-2], refs[-2:]
    total = share_refs[0][...].astype(jnp.float32)
    for share_ref in share_refs[1:]:
        total = total + share_ref[...].astype(jnp.float32)
    total = total.astype(jnp.bfloat16)
    for i in range(KV_WIDTH // span):
        own = slice(i * span, (i + 1) * span)
        dk_ref[0, :, own] = total[:, 2 * i * span : (2 * i + 1) * span]
        dv_ref[0, :, own] = total[:, (2 * i + 1) * span : (2 * i + 2) * span]


def fold_kernel(share_ref, out_ref):
    total = share_ref[0]
    for part in range(1, share_ref.shape[0]):
        total = total + share_ref[part]
    for part in range(out_ref.shape[0]):
        out_ref[part] = total


def fold(shares, parts, flops):
    return pl.pallas_call(
        fold_kernel,
        out_shape=jax.ShapeDtypeStruct((parts, *shares.shape[1:]), shares.dtype),
        compiler_params=params(),
        cost_estimate=pl.CostEstimate(flops=flops, bytes_accessed=4096, transcendentals=0),
        name="fold",
    )(shares)


def body(
    hidden_rows,
    chosen_query_rows,
    key_rows,
    chosen_value_rows,
    output_gradient,
    positions,
    counts,
    router,
):
    rows, width = chosen_query_rows.shape[1:]
    payload = pl.pallas_call(
        pack_kernel,
        out_shape=jax.ShapeDtypeStruct((Y, rows, 2 * KV_WIDTH + 128), jnp.bfloat16),
        in_specs=[HBM, HBM, HBM],
        out_specs=HBM,
        scratch_shapes=[
            pltpu.VMEM((1, rows), jnp.int32),
            pltpu.VMEM((rows, 2 * KV_WIDTH + 128), jnp.bfloat16),
            pltpu.SemaphoreType.DMA((3,)),
            pltpu.SemaphoreType.DMA((Y,)),
        ],
        compiler_params=params(FULL_VMEM),
        name="pack",
    )(key_rows, chosen_value_rows, positions)
    gathered = exchange(payload, "ctx", Y_FIRST)

    query_places = jnp.tile(positions, (1, GROUP))
    heads = 2
    steps = KEY_VALUE_HEADS // heads
    span = heads * HEAD_SIZE
    wide_block = pl.BlockSpec((1, rows, heads * GROUP * HEAD_SIZE), lambda i: (0, 0, i))
    key_block = pl.BlockSpec((Y, rows, span), lambda i: (0, 0, i))
    value_block = pl.BlockSpec((Y, rows, span), lambda i: (0, 0, i + steps))
    place_block = pl.BlockSpec((Y, rows, 128), lambda i: (0, 0, 2 * KEY_VALUE_HEADS))

    def whole(*shape):
        return pl.BlockSpec(shape, lambda i: (0,) * len(shape))

    along = pl.pallas_call(
        forward_kernel,
        out_shape=jax.ShapeDtypeStruct((rows, 128), jnp.float32),
        compiler_params=params(),
        cost_estimate=pl.CostEstimate(
            flops=4 * rows * width * Y * rows,
            bytes_accessed=6 * rows * width,
            transcendentals=rows * QUERY_HEADS * Y * rows,
        ),
        name="forward",
    )(chosen_query_rows, output_gradient, gathered, query_places)
    chunk = width // PLANE
    vmem = pl.BlockSpec(memory_space=pltpu.VMEM)
    term, gate = pl.pallas_call(
        router_kernel,
        out_shape=[
            jax.ShapeDtypeStruct((PLANE, 1, chunk), jnp.float32),
            jax.ShapeDtypeStruct((rows, 128), jnp.float32),
        ],
        in_specs=[vmem, vmem, vmem, pl.BlockSpec(memory_space=pltpu.SMEM)],
        compiler_params=params(),
        cost_estimate=pl.CostEstimate(
            flops=4 * rows * width, bytes_accessed=2 * rows * width, transcendentals=rows
        ),
        name="router",
    )(along, hidden_rows, router.reshape(1, width), counts)

    query_gradient, *terms = pl.pallas_call(
        functools.partial(backward_kernel, heads),
        grid=(steps,),
        out_shape=[
            jax.ShapeDtypeStruct((1, rows, width), jnp.bfloat16),
            *[jax.ShapeDtypeStruct((rows, 2 * KV_WIDTH), jnp.bfloat16)] * Y,
        ],
        in_specs=[
            wide_block,
            wide_block,
            key_block,
            value_block,
            place_block,
            whole(1, GROUP * rows),
            whole(rows, 128),
        ],
        out_specs=[wide_block] + [pl.BlockSpec((rows, 2 * span), lambda i: (0, i))] * Y,
        compiler_params=params(BACKWARD_VMEM),
        cost_estimate=pl.CostEstimate(
            flops=10 * rows * width * Y * rows,
            bytes_accessed=6 * rows * width,
            transcendentals=rows * QUERY_HEADS * Y * rows,
        ),
        name="backward",
    )(
        chosen_query_rows,
        output_gradient,
        gathered,
        gathered,
        gathered,
        query_places,
        gate,
    )

    plane = ("x", "core", "ctx")
    shares = exchange(term, plane, SUM_FIRST)
    share = fold(shares, Z, 8192)
    share, *terms = lax.optimization_barrier((share, *terms))
    lines = exchange(share, "z", Z_FIRST)
    term_shares = [terms[0]] + [
        lax.ppermute(terms[back], "ctx", [(i, i - back) for i in range(back, Y)])
        for back in range(1, Y)
    ]
    line = fold(lines, PLANE, FOLD_FLOPS)
    router_grad = exchange(line, plane, SPREAD_FIRST).reshape(width)
    key_gradient, value_gradient = pl.pallas_call(
        functools.partial(combine_kernel, span),
        out_shape=[jax.ShapeDtypeStruct((1, rows, KV_WIDTH), jnp.bfloat16)] * 2,
        compiler_params=params(),
        cost_estimate=pl.CostEstimate(
            flops=4 * rows * KV_WIDTH, bytes_accessed=20 * rows * KV_WIDTH, transcendentals=0
        ),
        name="combine",
    )(*term_shares)
    router_grad, key_gradient = lax.optimization_barrier((router_grad, key_gradient))
    return query_gradient, key_gradient, value_gradient, router_grad


def solution(mesh):
    fine = Mesh(mesh.devices.reshape(X, Z, CORES, Y), ("x", "z", "core", "ctx"))
    seq = ("x", "z", "core")
    rows3 = P(seq, "ctx", None)
    rows2 = P(seq, "ctx")
    return jax.shard_map(
        body,
        mesh=fine,
        in_specs=(rows3, rows3, rows3, rows3, rows3, rows2, rows2, P()),
        out_specs=(rows3, rows3, rows3, P()),
        check_vma=False,
    )
```

```python
import functools
import math

import jax
import jax.numpy as jnp
from jax import lax
from jax.experimental import pallas as pl
from jax.experimental.pallas import tpu as pltpu
from jax.sharding import Mesh, PartitionSpec as P

QUERY_HEADS = 64
KEY_VALUE_HEADS = 8
HEAD_SIZE = 128
GROUP = QUERY_HEADS // KEY_VALUE_HEADS
KV_WIDTH = KEY_VALUE_HEADS * HEAD_SIZE
SCALE = 1.0 / math.sqrt(HEAD_SIZE)
LOG2_SCALE = SCALE * math.log2(math.e)
X, Z, CORES, Y = 4, 16, 2, 4
PLANE = X * CORES * Y
Y_FIRST, Z_FIRST, SUM_FIRST, SPREAD_FIRST = 0, 11, 17, 19
VMEM_LIMIT = 48 * 1024 * 1024
FULL_VMEM = 60 * 1024 * 1024
BACKWARD_VMEM = 53 * 1024 * 1024
FOLD_FLOPS = 1 << 35
HBM = pl.BlockSpec(memory_space=pltpu.HBM)
NT = (((1,), (1,)), ((), ()))
TN = (((0,), (0,)), ((), ()))
NN = (((1,), (0,)), ((), ()))


def dot(a, b, dims):
    return lax.dot_general(a, b, dims, preferred_element_type=jnp.float32)


def exchange(parts, axis, first):
    size = parts.shape[0]
    order = [(i + first) % size for i in range(size)]
    return lax.all_to_all(parts, axis, 0, 0, axis_index_groups=[order], tiled=True)


def params(limit=VMEM_LIMIT):
    return pltpu.CompilerParams(vmem_limit_bytes=limit)


def column(row, rows):
    wide = jnp.broadcast_to(row, (rows, rows))
    diagonal = lax.broadcasted_iota(jnp.int32, (rows, rows), 0) == lax.broadcasted_iota(
        jnp.int32, (rows, rows), 1
    )
    return jnp.sum(jnp.where(diagonal, wide.astype(jnp.float32), 0.0), axis=1, keepdims=True)


def pack_kernel(key_ref, value_ref, place_ref, out_ref, row_ref, block_ref, in_sems, out_sems):
    rows = key_ref.shape[1]
    fetches = [
        pltpu.make_async_copy(place_ref, row_ref, in_sems.at[0]),
        pltpu.make_async_copy(key_ref.at[0], block_ref.at[:, :KV_WIDTH], in_sems.at[1]),
        pltpu.make_async_copy(
            value_ref.at[0], block_ref.at[:, KV_WIDTH : 2 * KV_WIDTH], in_sems.at[2]
        ),
    ]
    for fetch in fetches:
        fetch.start()
    fetches[0].wait()
    places = column(row_ref[...], rows)
    high = jnp.floor(places * (1.0 / 16.0))
    low = places - 16.0 * high
    lane = lax.broadcasted_iota(jnp.int32, (rows, 128), 1)
    coded = jnp.where(lane == 0, high, jnp.where(lane == 1, low, 0.0))
    block_ref[:, 2 * KV_WIDTH :] = coded.astype(jnp.bfloat16)
    fetches[1].wait()
    fetches[2].wait()
    copies = [
        pltpu.make_async_copy(block_ref, out_ref.at[part], out_sems.at[part]) for part in range(Y)
    ]
    for copy in copies:
        copy.start()
    for copy in copies:
        copy.wait()


def key_places(place_block):
    coded = place_block.reshape(-1, 128).astype(jnp.float32)
    return coded[:, 0:1] * 16.0 + coded[:, 1:2]


def stack_heads(block, first, rows):
    return jnp.concatenate(
        [block[:, (first + g) * HEAD_SIZE : (first + g + 1) * HEAD_SIZE] for g in range(GROUP)],
        axis=0,
    )


def mask_bias(places, query_places):
    return jnp.where(places <= query_places.astype(jnp.float32), 0.0, -1e30)


def weights_of(scores, bias):
    scores = scores + jnp.concatenate([bias] * (scores.shape[1] // bias.shape[1]), axis=1)
    top = jnp.max(scores, axis=0, keepdims=True)
    weights = jnp.exp2((scores - top) * LOG2_SCALE)
    return weights, jnp.sum(weights, axis=0, keepdims=True)


def forward_kernel(q_ref, grad_ref, pay_ref, qp_ref, out_ref):
    rows = q_ref.shape[1]
    bias = mask_bias(key_places(pay_ref[:, :, 2 * KV_WIDTH :]), qp_ref[:, : 2 * rows])

    acc = jnp.zeros((1, GROUP * rows), jnp.float32)
    for c in range(KEY_VALUE_HEADS):
        left = c * HEAD_SIZE
        queries = stack_heads(q_ref[0], c * GROUP, rows)
        keys = pay_ref[:, :, left : left + HEAD_SIZE].reshape(-1, HEAD_SIZE)
        weights, total = weights_of(dot(keys, queries, NT), bias)
        left = left + KV_WIDTH
        grads = stack_heads(grad_ref[0], c * GROUP, rows)
        values = pay_ref[:, :, left : left + HEAD_SIZE].reshape(-1, HEAD_SIZE)
        along = dot(values, grads, NT)
        acc = acc + jnp.sum(weights * along, axis=0, keepdims=True) / total
    row_sum = acc[:, :rows]
    for g in range(1, GROUP):
        row_sum = row_sum + acc[:, g * rows : (g + 1) * rows]
    wide = jnp.broadcast_to(row_sum, (rows, rows))
    diagonal = lax.broadcasted_iota(jnp.int32, (rows, rows), 0) == lax.broadcasted_iota(
        jnp.int32, (rows, rows), 1
    )
    down = jnp.sum(jnp.where(diagonal, wide, 0.0), axis=1, keepdims=True)
    out_ref[...] = jnp.broadcast_to(down, (rows, 128))


def router_kernel(along_ref, hidden_ref, router_ref, count_ref, out_ref, gate_ref):
    rows, width = hidden_ref.shape[1:]
    total = jnp.zeros((rows, 128), jnp.float32)
    for left in range(0, width, 128):
        block = hidden_ref[0, :, left : left + 128].astype(jnp.float32)
        total = total + block * router_ref[:, left : left + 128]
    sigma = jax.nn.sigmoid(jnp.sum(total, axis=1, keepdims=True))
    slot = lax.broadcasted_iota(jnp.int32, (rows, 1), 0)
    valid = (slot < count_ref[0, 0]).astype(jnp.float32)
    gate_ref[...] = jnp.broadcast_to(sigma * valid, (rows, 128))
    slope = sigma * (1.0 - sigma) * valid
    logit_grad = along_ref[...] * slope * (1.0 / math.sqrt(X * Z * CORES * Y * rows))
    chunk = out_ref.shape[2]
    for part in range(PLANE):
        column = (part + SUM_FIRST - SPREAD_FIRST) % PLANE * chunk
        for lane in range(0, chunk, 128):
            left = column + lane
            block = hidden_ref[0, :, left : left + 128].astype(jnp.float32)
            out_ref[part, :, lane : lane + 128] = jnp.sum(
                block * logit_grad, axis=0, keepdims=True
            )


def backward_kernel(
    heads,
    q_ref,
    grad_ref,
    k_ref,
    v_ref,
    kp_ref,
    qp_ref,
    gate_ref,
    dq_ref,
    *term_refs,
):
    rows = q_ref.shape[1]
    me = lax.axis_index("ctx")
    owners = [lax.rem(me + 2 * Y - back - Y_FIRST, Y) for back in range(Y)]

    def blocks(ref, columns):
        return jnp.concatenate([ref[owner, :, columns] for owner in owners], axis=0)

    bias = mask_bias(key_places(blocks(kp_ref, slice(0, 128))), qp_ref[:, : 2 * rows])
    gate = gate_ref[:, :1]
    for c in range(heads):
        queries = stack_heads(q_ref[0], c * GROUP, rows)
        grads = jnp.concatenate(
            [
                (
                    grad_ref[
                        0, :, (c * GROUP + g) * HEAD_SIZE : (c * GROUP + g + 1) * HEAD_SIZE
                    ].astype(jnp.float32)
                    * gate
                ).astype(jnp.bfloat16)
                for g in range(GROUP)
            ],
            axis=0,
        )
        own = slice(c * HEAD_SIZE, (c + 1) * HEAD_SIZE)
        beside = slice((heads + c) * HEAD_SIZE, (heads + c + 1) * HEAD_SIZE)
        keys = blocks(k_ref, own)
        values = blocks(v_ref, own)
        weights, total = weights_of(dot(keys, queries, NT), bias)
        probs = (weights * (1.0 / total)).astype(jnp.bfloat16)
        probs32 = probs.astype(jnp.float32)
        grad_probs = dot(values, grads, NT)
        row_dot = jnp.sum(probs32 * grad_probs, axis=0, keepdims=True)
        grad_scores = (probs32 * (grad_probs - row_dot)).astype(jnp.bfloat16)
        dv = dot(probs, grads, NN).astype(jnp.bfloat16)
        dk = (dot(grad_scores, queries, NN) * SCALE).astype(jnp.bfloat16)
        dq = (dot(grad_scores, keys, TN) * SCALE).astype(jnp.bfloat16)
        for back, term_ref in enumerate(term_refs):
            term_ref[:, own] = dk[back * rows : (back + 1) * rows]
            term_ref[:, beside] = dv[back * rows : (back + 1) * rows]
        for g in range(GROUP):
            left = (c * GROUP + g) * HEAD_SIZE
            dq_ref[0, :, left : left + HEAD_SIZE] = dq[g * rows : (g + 1) * rows]


def combine_kernel(span, *refs):
    share_refs, (dk_ref, dv_ref) = refs[:-2], refs[-2:]
    total = share_refs[0][...].astype(jnp.float32)
    for share_ref in share_refs[1:]:
        total = total + share_ref[...].astype(jnp.float32)
    total = total.astype(jnp.bfloat16)
    for i in range(KV_WIDTH // span):
        own = slice(i * span, (i + 1) * span)
        dk_ref[0, :, own] = total[:, 2 * i * span : (2 * i + 1) * span]
        dv_ref[0, :, own] = total[:, (2 * i + 1) * span : (2 * i + 2) * span]


def fold_kernel(share_ref, out_ref):
    total = share_ref[0]
    for part in range(1, share_ref.shape[0]):
        total = total + share_ref[part]
    for part in range(out_ref.shape[0]):
        out_ref[part] = total


def fold(shares, parts, flops):
    return pl.pallas_call(
        fold_kernel,
        out_shape=jax.ShapeDtypeStruct((parts, *shares.shape[1:]), shares.dtype),
        compiler_params=params(),
        cost_estimate=pl.CostEstimate(flops=flops, bytes_accessed=4096, transcendentals=0),
        name="fold",
    )(shares)


def body(
    hidden_rows,
    chosen_query_rows,
    key_rows,
    chosen_value_rows,
    output_gradient,
    positions,
    counts,
    router,
):
    rows, width = chosen_query_rows.shape[1:]
    payload = pl.pallas_call(
        pack_kernel,
        out_shape=jax.ShapeDtypeStruct((Y, rows, 2 * KV_WIDTH + 128), jnp.bfloat16),
        in_specs=[HBM, HBM, HBM],
        out_specs=HBM,
        scratch_shapes=[
            pltpu.VMEM((1, rows), jnp.int32),
            pltpu.VMEM((rows, 2 * KV_WIDTH + 128), jnp.bfloat16),
            pltpu.SemaphoreType.DMA((3,)),
            pltpu.SemaphoreType.DMA((Y,)),
        ],
        compiler_params=params(FULL_VMEM),
        name="pack",
    )(key_rows, chosen_value_rows, positions)
    gathered = exchange(payload, "ctx", Y_FIRST)

    query_places = jnp.tile(positions, (1, GROUP))
    heads = 4
    steps = KEY_VALUE_HEADS // heads
    span = heads * HEAD_SIZE
    wide_block = pl.BlockSpec((1, rows, heads * GROUP * HEAD_SIZE), lambda i: (0, 0, i))
    key_block = pl.BlockSpec((Y, rows, span), lambda i: (0, 0, i))
    value_block = pl.BlockSpec((Y, rows, span), lambda i: (0, 0, i + steps))
    place_block = pl.BlockSpec((Y, rows, 128), lambda i: (0, 0, 2 * KEY_VALUE_HEADS))

    def whole(*shape):
        return pl.BlockSpec(shape, lambda i: (0,) * len(shape))

    along = pl.pallas_call(
        forward_kernel,
        out_shape=jax.ShapeDtypeStruct((rows, 128), jnp.float32),
        compiler_params=params(),
        cost_estimate=pl.CostEstimate(
            flops=4 * rows * width * Y * rows,
            bytes_accessed=6 * rows * width,
            transcendentals=rows * QUERY_HEADS * Y * rows,
        ),
        name="forward",
    )(chosen_query_rows, output_gradient, gathered, query_places)
    chunk = width // PLANE
    vmem = pl.BlockSpec(memory_space=pltpu.VMEM)
    term, gate = pl.pallas_call(
        router_kernel,
        out_shape=[
            jax.ShapeDtypeStruct((PLANE, 1, chunk), jnp.float32),
            jax.ShapeDtypeStruct((rows, 128), jnp.float32),
        ],
        in_specs=[vmem, vmem, vmem, pl.BlockSpec(memory_space=pltpu.SMEM)],
        compiler_params=params(),
        cost_estimate=pl.CostEstimate(
            flops=4 * rows * width, bytes_accessed=2 * rows * width, transcendentals=rows
        ),
        name="router",
    )(along, hidden_rows, router.reshape(1, width), counts)

    query_gradient, *terms = pl.pallas_call(
        functools.partial(backward_kernel, heads),
        grid=(steps,),
        out_shape=[
            jax.ShapeDtypeStruct((1, rows, width), jnp.bfloat16),
            *[jax.ShapeDtypeStruct((rows, 2 * KV_WIDTH), jnp.bfloat16)] * Y,
        ],
        in_specs=[
            wide_block,
            wide_block,
            key_block,
            value_block,
            place_block,
            whole(1, GROUP * rows),
            whole(rows, 128),
        ],
        out_specs=[wide_block] + [pl.BlockSpec((rows, 2 * span), lambda i: (0, i))] * Y,
        compiler_params=params(BACKWARD_VMEM),
        cost_estimate=pl.CostEstimate(
            flops=10 * rows * width * Y * rows,
            bytes_accessed=6 * rows * width,
            transcendentals=rows * QUERY_HEADS * Y * rows,
        ),
        name="backward",
    )(
        chosen_query_rows,
        output_gradient,
        gathered,
        gathered,
        gathered,
        query_places,
        gate,
    )

    plane = ("x", "core", "ctx")
    shares = exchange(term, plane, SUM_FIRST)
    share = fold(shares, Z, 8192)
    share, *terms = lax.optimization_barrier((share, *terms))
    lines = exchange(share, "z", Z_FIRST)
    term_shares = [terms[0]] + [
        lax.ppermute(terms[back], "ctx", [(i, i - back) for i in range(back, Y)])
        for back in (2, 3, 1)
    ]
    line = fold(lines, PLANE, FOLD_FLOPS)
    router_grad = exchange(line, plane, SPREAD_FIRST).reshape(width)
    key_gradient, value_gradient = pl.pallas_call(
        functools.partial(combine_kernel, span),
        out_shape=[jax.ShapeDtypeStruct((1, rows, KV_WIDTH), jnp.bfloat16)] * 2,
        compiler_params=params(),
        cost_estimate=pl.CostEstimate(
            flops=4 * rows * KV_WIDTH, bytes_accessed=20 * rows * KV_WIDTH, transcendentals=0
        ),
        name="combine",
    )(*term_shares)
    router_grad, key_gradient = lax.optimization_barrier((router_grad, key_gradient))
    return query_gradient, key_gradient, value_gradient, router_grad


def solution(mesh):
    fine = Mesh(mesh.devices.reshape(X, Z, CORES, Y), ("x", "z", "core", "ctx"))
    seq = ("x", "z", "core")
    rows3 = P(seq, "ctx", None)
    rows2 = P(seq, "ctx")
    return jax.shard_map(
        body,
        mesh=fine,
        in_specs=(rows3, rows3, rows3, rows3, rows3, rows2, rows2, P()),
        out_specs=(rows3, rows3, rows3, P()),
        check_vma=False,
    )
```

```python
import functools
import math

import jax
import jax.numpy as jnp
from jax import lax
from jax.experimental import pallas as pl
from jax.experimental.pallas import tpu as pltpu
from jax.sharding import Mesh, PartitionSpec as P

QUERY_HEADS = 64
KEY_VALUE_HEADS = 8
HEAD_SIZE = 128
GROUP = QUERY_HEADS // KEY_VALUE_HEADS
KV_WIDTH = KEY_VALUE_HEADS * HEAD_SIZE
SCALE = 1.0 / math.sqrt(HEAD_SIZE)
LOG2_SCALE = SCALE * math.log2(math.e)
X, Z, CORES, Y = 4, 16, 2, 4
PLANE = X * CORES * Y
Y_FIRST, Z_FIRST, SUM_FIRST, SPREAD_FIRST = 0, 11, 17, 19
VMEM_LIMIT = 48 * 1024 * 1024
FULL_VMEM = 60 * 1024 * 1024
BACKWARD_VMEM = 53 * 1024 * 1024
FOLD_FLOPS = 1 << 35
HBM = pl.BlockSpec(memory_space=pltpu.HBM)
NT = (((1,), (1,)), ((), ()))
TN = (((0,), (0,)), ((), ()))
NN = (((1,), (0,)), ((), ()))


def dot(a, b, dims):
    return lax.dot_general(a, b, dims, preferred_element_type=jnp.float32)


def exchange(parts, axis, first):
    size = parts.shape[0]
    order = [(i + first) % size for i in range(size)]
    return lax.all_to_all(parts, axis, 0, 0, axis_index_groups=[order], tiled=True)


def params(limit=VMEM_LIMIT):
    return pltpu.CompilerParams(vmem_limit_bytes=limit)


def column(row, rows):
    wide = jnp.broadcast_to(row, (rows, rows))
    diagonal = lax.broadcasted_iota(jnp.int32, (rows, rows), 0) == lax.broadcasted_iota(
        jnp.int32, (rows, rows), 1
    )
    return jnp.sum(jnp.where(diagonal, wide.astype(jnp.float32), 0.0), axis=1, keepdims=True)


def pack_kernel(key_ref, value_ref, place_ref, out_ref, row_ref, block_ref, in_sems, out_sems):
    rows = key_ref.shape[1]
    half = rows // 2
    fetches = [pltpu.make_async_copy(place_ref, row_ref, in_sems.at[0])]
    for top in (0, half):
        for i, source in enumerate((key_ref, value_ref)):
            target = block_ref.at[top : top + half, i * KV_WIDTH : (i + 1) * KV_WIDTH]
            fetches.append(
                pltpu.make_async_copy(
                    source.at[0, top : top + half], target, in_sems.at[len(fetches)]
                )
            )
    for fetch in fetches:
        fetch.start()
    fetches[0].wait()
    places = column(row_ref[...], rows)
    high = jnp.floor(places * (1.0 / 16.0))
    low = places - 16.0 * high
    lane = lax.broadcasted_iota(jnp.int32, (rows, 128), 1)
    coded = jnp.where(lane == 0, high, jnp.where(lane == 1, low, 0.0))
    block_ref[:, 2 * KV_WIDTH :] = coded.astype(jnp.bfloat16)
    copies = []
    for step, top in enumerate((0, half)):
        fetches[1 + 2 * step].wait()
        fetches[2 + 2 * step].wait()
        for part in range(Y):
            source = block_ref.at[top : top + half]
            target = out_ref.at[part, top : top + half]
            copies.append(pltpu.make_async_copy(source, target, out_sems.at[step, part]))
            copies[-1].start()
    for copy in copies:
        copy.wait()


def key_places(place_block):
    coded = place_block.reshape(-1, 128).astype(jnp.float32)
    return coded[:, 0:1] * 16.0 + coded[:, 1:2]


def stack_heads(block, first, rows):
    return jnp.concatenate(
        [block[:, (first + g) * HEAD_SIZE : (first + g + 1) * HEAD_SIZE] for g in range(GROUP)],
        axis=0,
    )


def mask_bias(places, query_places):
    return jnp.where(places <= query_places.astype(jnp.float32), 0.0, -1e30)


def weights_of(scores, bias):
    scores = scores + jnp.concatenate([bias] * (scores.shape[1] // bias.shape[1]), axis=1)
    top = jnp.max(scores, axis=0, keepdims=True)
    weights = jnp.exp2((scores - top) * LOG2_SCALE)
    return weights, jnp.sum(weights, axis=0, keepdims=True)


def forward_kernel(q_ref, grad_ref, pay_ref, qp_ref, out_ref):
    rows = q_ref.shape[1]
    bias = mask_bias(key_places(pay_ref[:, :, 2 * KV_WIDTH :]), qp_ref[:, : 2 * rows])

    acc = jnp.zeros((1, GROUP * rows), jnp.float32)
    for c in range(KEY_VALUE_HEADS):
        left = c * HEAD_SIZE
        queries = stack_heads(q_ref[0], c * GROUP, rows)
        keys = pay_ref[:, :, left : left + HEAD_SIZE].reshape(-1, HEAD_SIZE)
        weights, total = weights_of(dot(keys, queries, NT), bias)
        left = left + KV_WIDTH
        grads = stack_heads(grad_ref[0], c * GROUP, rows)
        values = pay_ref[:, :, left : left + HEAD_SIZE].reshape(-1, HEAD_SIZE)
        along = dot(values, grads, NT)
        acc = acc + jnp.sum(weights * along, axis=0, keepdims=True) / total
    row_sum = acc[:, :rows]
    for g in range(1, GROUP):
        row_sum = row_sum + acc[:, g * rows : (g + 1) * rows]
    wide = jnp.broadcast_to(row_sum, (rows, rows))
    diagonal = lax.broadcasted_iota(jnp.int32, (rows, rows), 0) == lax.broadcasted_iota(
        jnp.int32, (rows, rows), 1
    )
    down = jnp.sum(jnp.where(diagonal, wide, 0.0), axis=1, keepdims=True)
    out_ref[...] = jnp.broadcast_to(down, (rows, 128))


def router_kernel(along_ref, hidden_ref, router_ref, count_ref, out_ref, gate_ref):
    rows, width = hidden_ref.shape[1:]
    total = jnp.zeros((rows, 128), jnp.float32)
    for left in range(0, width, 128):
        block = hidden_ref[0, :, left : left + 128].astype(jnp.float32)
        total = total + block * router_ref[:, left : left + 128]
    sigma = jax.nn.sigmoid(jnp.sum(total, axis=1, keepdims=True))
    slot = lax.broadcasted_iota(jnp.int32, (rows, 1), 0)
    valid = (slot < count_ref[0, 0]).astype(jnp.float32)
    gate_ref[...] = jnp.broadcast_to(sigma * valid, (rows, 128))
    slope = sigma * (1.0 - sigma) * valid
    logit_grad = along_ref[...] * slope * (1.0 / math.sqrt(X * Z * CORES * Y * rows))
    chunk = out_ref.shape[2]
    for part in range(PLANE):
        column = (part + SUM_FIRST - SPREAD_FIRST) % PLANE * chunk
        for lane in range(0, chunk, 128):
            left = column + lane
            block = hidden_ref[0, :, left : left + 128].astype(jnp.float32)
            out_ref[part, :, lane : lane + 128] = jnp.sum(
                block * logit_grad, axis=0, keepdims=True
            )


def backward_kernel(
    heads,
    q_ref,
    grad_ref,
    k_ref,
    v_ref,
    kp_ref,
    qp_ref,
    gate_ref,
    dq_ref,
    *refs,
):
    *term_refs, bias_ref = refs
    rows = q_ref.shape[1]
    me = lax.axis_index("ctx")
    owners = [lax.rem(me + 2 * Y - back - Y_FIRST, Y) for back in range(Y)]

    def blocks(ref, columns):
        return jnp.concatenate([ref[owner, :, columns] for owner in owners], axis=0)

    @pl.when(pl.program_id(0) == 0)
    def _():
        bias_ref[...] = mask_bias(key_places(blocks(kp_ref, slice(0, 128))), qp_ref[:, : 2 * rows])

    bias = bias_ref[...]
    gate = gate_ref[:, :1]
    for c in range(heads):
        queries = stack_heads(q_ref[0], c * GROUP, rows)
        grads = jnp.concatenate(
            [
                (
                    grad_ref[
                        0, :, (c * GROUP + g) * HEAD_SIZE : (c * GROUP + g + 1) * HEAD_SIZE
                    ].astype(jnp.float32)
                    * gate
                ).astype(jnp.bfloat16)
                for g in range(GROUP)
            ],
            axis=0,
        )
        own = slice(c * HEAD_SIZE, (c + 1) * HEAD_SIZE)
        beside = slice((heads + c) * HEAD_SIZE, (heads + c + 1) * HEAD_SIZE)
        keys = blocks(k_ref, own)
        values = blocks(v_ref, own)
        weights, total = weights_of(dot(keys, queries, NT), bias)
        probs = (weights * (1.0 / total)).astype(jnp.bfloat16)
        probs32 = probs.astype(jnp.float32)
        grad_probs = dot(values, grads, NT)
        row_dot = jnp.sum(probs32 * grad_probs, axis=0, keepdims=True)
        grad_scores = (probs32 * (grad_probs - row_dot)).astype(jnp.bfloat16)
        dv = dot(probs, grads, NN).astype(jnp.bfloat16)
        dk = (dot(grad_scores, queries, NN) * SCALE).astype(jnp.bfloat16)
        dq = (dot(grad_scores, keys, TN) * SCALE).astype(jnp.bfloat16)
        for back, term_ref in enumerate(term_refs):
            term_ref[:, own] = dk[back * rows : (back + 1) * rows]
            term_ref[:, beside] = dv[back * rows : (back + 1) * rows]
        for g in range(GROUP):
            left = (c * GROUP + g) * HEAD_SIZE
            dq_ref[0, :, left : left + HEAD_SIZE] = dq[g * rows : (g + 1) * rows]


def combine_kernel(span, *refs):
    share_refs, (dk_ref, dv_ref) = refs[:-2], refs[-2:]
    total = share_refs[0][...].astype(jnp.float32)
    for share_ref in share_refs[1:]:
        total = total + share_ref[...].astype(jnp.float32)
    total = total.astype(jnp.bfloat16)
    for i in range(KV_WIDTH // span):
        own = slice(i * span, (i + 1) * span)
        dk_ref[0, :, own] = total[:, 2 * i * span : (2 * i + 1) * span]
        dv_ref[0, :, own] = total[:, (2 * i + 1) * span : (2 * i + 2) * span]


def fold_kernel(share_ref, out_ref):
    total = share_ref[0]
    for part in range(1, share_ref.shape[0]):
        total = total + share_ref[part]
    for part in range(out_ref.shape[0]):
        out_ref[part] = total


def fold(shares, parts, flops):
    return pl.pallas_call(
        fold_kernel,
        out_shape=jax.ShapeDtypeStruct((parts, *shares.shape[1:]), shares.dtype),
        compiler_params=params(),
        cost_estimate=pl.CostEstimate(flops=flops, bytes_accessed=4096, transcendentals=0),
        name="fold",
    )(shares)


def body(
    hidden_rows,
    chosen_query_rows,
    key_rows,
    chosen_value_rows,
    output_gradient,
    positions,
    counts,
    router,
):
    rows, width = chosen_query_rows.shape[1:]
    payload = pl.pallas_call(
        pack_kernel,
        out_shape=jax.ShapeDtypeStruct((Y, rows, 2 * KV_WIDTH + 128), jnp.bfloat16),
        in_specs=[HBM, HBM, HBM],
        out_specs=HBM,
        scratch_shapes=[
            pltpu.VMEM((1, rows), jnp.int32),
            pltpu.VMEM((rows, 2 * KV_WIDTH + 128), jnp.bfloat16),
            pltpu.SemaphoreType.DMA((5,)),
            pltpu.SemaphoreType.DMA((2, Y)),
        ],
        compiler_params=params(FULL_VMEM),
        name="pack",
    )(key_rows, chosen_value_rows, positions)
    gathered = exchange(payload, "ctx", Y_FIRST)

    query_places = jnp.tile(positions, (1, GROUP))
    heads = 4
    steps = KEY_VALUE_HEADS // heads
    span = heads * HEAD_SIZE
    wide_block = pl.BlockSpec((1, rows, heads * GROUP * HEAD_SIZE), lambda i: (0, 0, i))
    key_block = pl.BlockSpec((Y, rows, span), lambda i: (0, 0, i))
    value_block = pl.BlockSpec((Y, rows, span), lambda i: (0, 0, i + steps))
    place_block = pl.BlockSpec((Y, rows, 128), lambda i: (0, 0, 2 * KEY_VALUE_HEADS))

    def whole(*shape):
        return pl.BlockSpec(shape, lambda i: (0,) * len(shape))

    along = pl.pallas_call(
        forward_kernel,
        out_shape=jax.ShapeDtypeStruct((rows, 128), jnp.float32),
        compiler_params=params(),
        cost_estimate=pl.CostEstimate(
            flops=4 * rows * width * Y * rows,
            bytes_accessed=6 * rows * width,
            transcendentals=rows * QUERY_HEADS * Y * rows,
        ),
        name="forward",
    )(chosen_query_rows, output_gradient, gathered, query_places)
    chunk = width // PLANE
    vmem = pl.BlockSpec(memory_space=pltpu.VMEM)
    term, gate = pl.pallas_call(
        router_kernel,
        out_shape=[
            jax.ShapeDtypeStruct((PLANE, 1, chunk), jnp.float32),
            jax.ShapeDtypeStruct((rows, 128), jnp.float32),
        ],
        in_specs=[vmem, vmem, vmem, pl.BlockSpec(memory_space=pltpu.SMEM)],
        compiler_params=params(),
        cost_estimate=pl.CostEstimate(
            flops=4 * rows * width, bytes_accessed=2 * rows * width, transcendentals=rows
        ),
        name="router",
    )(along, hidden_rows, router.reshape(1, width), counts)

    query_gradient, *terms = pl.pallas_call(
        functools.partial(backward_kernel, heads),
        grid=(steps,),
        out_shape=[
            jax.ShapeDtypeStruct((1, rows, width), jnp.bfloat16),
            *[jax.ShapeDtypeStruct((rows, 2 * KV_WIDTH), jnp.bfloat16)] * Y,
        ],
        in_specs=[
            wide_block,
            wide_block,
            key_block,
            value_block,
            place_block,
            whole(1, GROUP * rows),
            whole(rows, 128),
        ],
        out_specs=[wide_block] + [pl.BlockSpec((rows, 2 * span), lambda i: (0, i))] * Y,
        scratch_shapes=[pltpu.VMEM((Y * rows, 2 * rows), jnp.float32)],
        compiler_params=params(BACKWARD_VMEM),
        cost_estimate=pl.CostEstimate(
            flops=10 * rows * width * Y * rows,
            bytes_accessed=6 * rows * width,
            transcendentals=rows * QUERY_HEADS * Y * rows,
        ),
        name="backward",
    )(
        chosen_query_rows,
        output_gradient,
        gathered,
        gathered,
        gathered,
        query_places,
        gate,
    )

    plane = ("x", "core", "ctx")
    shares = exchange(term, plane, SUM_FIRST)
    share = fold(shares, Z, 8192)
    share, *terms = lax.optimization_barrier((share, *terms))
    lines = exchange(share, "z", Z_FIRST)
    term_shares = [terms[0]] + [
        lax.ppermute(terms[back], "ctx", [(i, i - back) for i in range(back, Y)])
        for back in (2, 3, 1)
    ]
    line = fold(lines, PLANE, FOLD_FLOPS)
    router_grad = exchange(line, plane, SPREAD_FIRST).reshape(width)
    key_gradient, value_gradient = pl.pallas_call(
        functools.partial(combine_kernel, span),
        out_shape=[jax.ShapeDtypeStruct((1, rows, KV_WIDTH), jnp.bfloat16)] * 2,
        compiler_params=params(),
        cost_estimate=pl.CostEstimate(
            flops=4 * rows * KV_WIDTH, bytes_accessed=20 * rows * KV_WIDTH, transcendentals=0
        ),
        name="combine",
    )(*term_shares)
    router_grad, key_gradient = lax.optimization_barrier((router_grad, key_gradient))
    return query_gradient, key_gradient, value_gradient, router_grad


def solution(mesh):
    fine = Mesh(mesh.devices.reshape(X, Z, CORES, Y), ("x", "z", "core", "ctx"))
    seq = ("x", "z", "core")
    rows3 = P(seq, "ctx", None)
    rows2 = P(seq, "ctx")
    return jax.shard_map(
        body,
        mesh=fine,
        in_specs=(rows3, rows3, rows3, rows3, rows3, rows2, rows2, P()),
        out_specs=(rows3, rows3, rows3, P()),
        check_vma=False,
    )
```
